128 devices in a mesh: section: 4 (over z_lo, core), blk: 32 (over x, y, z_hi).
Axes of the slice: x: 4, y: 4, z: 4 (z_hi: 2, z_lo: 2; z = z_hi * 2 + z_lo), core: 2. Of those that a mesh axis runs over, the one named last changes fastest.
Arguments:
- queries: bfloat16 [4, 4096, 4096], P('section', 'blk'), may hold values from -200 to 200
- out_grad: bfloat16 [4, 4096, 4096], P('section', 'blk'), may hold values from -6 to 6
- kv_codes: int32 [2, 4096, 1024], P(None, 'blk', 'section'), may hold values from -127 to 127, as said below
- kv_scales: float32 [2, 128, 8], P(None, 'blk', 'section'), may hold values from 0.005 to 0.012
Outputs:
- query_grad: bfloat16 [4, 4096, 4096], P('section', 'blk')
- kv_grad: float32 [2, 4096, 1024], P(None, 'blk', 'section')
The draws below stay inside these ranges and needn't reach their ends.
Inputs may be any that keep to these rules, and one draw needn't show every extreme that they name: `kv_codes`: whole numbers.
All inputs are finite; a program needn't handle non-finite values.
Results may differ from the reference program's by a relative error of at most 0.03.
Values may be sent and summed in bfloat16 or wider, within the bound.
No kernel may reach another device: no remote copies, remote signals or barrier semaphores. Data moves between devices by JAX's collectives and lax.ppermute only.
A program may use at most 128 MiB of HBM per device.

```python
import jax
import jax.numpy as jnp
from jax import lax

HEADS = 32
KV_HEADS = 8
HEAD_DIM = 128
QUANT_BLOCK = 32
TOK_DEV = 128
TOKENS = 4096
SECTIONS = 4
N_BLK = 32


def cache_codes(key):
    inner = jax.random.fold_in(key, 101)
    return jax.random.randint(inner, (2, TOKENS, KV_HEADS * HEAD_DIM), -127, 128, dtype=jnp.int32)


def cache_scales(key):
    inner = jax.random.fold_in(key, 202)
    spread = jax.random.uniform(inner, (2, TOKENS // QUANT_BLOCK, KV_HEADS), jnp.float32)
    return jnp.exp(jnp.log(0.005) + spread * jnp.log(2.4))


def draw_kv_codes(key, part):
    return cache_codes(key)


def draw_kv_scales(key, part):
    return cache_scales(key)


def draw_queries(key, part):
    key = jax.random.fold_in(key, 3)
    width = HEADS * HEAD_DIM
    values = jnp.clip(3.0 * jax.random.normal(key, (SECTIONS, TOKENS, width), jnp.float32), -200.0, 200.0)
    return values.astype(jnp.bfloat16)


def shard_levels(stream_key, shape, cuts, smallest, high):
    factor_of, own = 1.0, jax.random.fold_in(stream_key, 6)
    for axis_at, parts in cuts:
        heights = jnp.exp(jax.random.uniform(jax.random.fold_in(own, axis_at), (parts,), jnp.float32, smallest / len(cuts), high / len(cuts)))
        factor_of = factor_of * jnp.repeat(heights, shape[axis_at] // parts).reshape([-1 if axis == axis_at else 1 for axis in range(len(shape))])
    return factor_of


def scatter_about(stream_key, dims, deviation, most, cuts=(), held_as=jnp.bfloat16):
    result = jax.random.normal(stream_key, dims, jnp.float32) * deviation
    if len(cuts) > 0:
        result = shard_levels(stream_key, dims, cuts, -0.22, 0.18) * result
    return jnp.clip(result, min=-most, max=most).astype(held_as)


def setup_inputs(seed: int = 0) -> dict:
    arg_keys = jax.random.split(jax.random.key(seed), 5)
    queries = draw_queries(jax.random.fold_in(arg_keys[4], 71), 0)
    out_grad = scatter_about(arg_keys[1], (SECTIONS, TOKENS, HEADS * HEAD_DIM), 1.0, 6.0, ((0, 4), (1, 32)))
    kv_codes = draw_kv_codes(jax.random.fold_in(arg_keys[4], 71), 0)
    kv_scales = draw_kv_scales(jax.random.fold_in(arg_keys[4], 71), 0)
    return {"queries": queries, "out_grad": out_grad, "kv_codes": kv_codes, "kv_scales": kv_scales}


def dequantize(kv_codes, kv_scales):
    per_entry = jnp.repeat(jnp.repeat(kv_scales, QUANT_BLOCK, axis=1), HEAD_DIM, axis=2)
    return (kv_codes.astype(jnp.float32) * per_entry).astype(jnp.bfloat16)


def shard_grads(query_rows, cotangent_rows, cache, first_row):
    groups = HEADS // KV_HEADS
    inv_scale = 1.0 / (HEAD_DIM ** 0.5)
    query_heads = query_rows.reshape(TOK_DEV, KV_HEADS, groups, HEAD_DIM).astype(jnp.float32)
    cotangent = cotangent_rows.reshape(TOK_DEV, KV_HEADS, groups, HEAD_DIM).astype(jnp.float32)
    key_rows = cache[0].reshape(TOKENS, KV_HEADS, HEAD_DIM).astype(jnp.float32)
    value_rows = cache[1].reshape(TOKENS, KV_HEADS, HEAD_DIM).astype(jnp.float32)
    scores = jnp.einsum("ihgd,jhd->hgij", query_heads, key_rows) * inv_scale
    row_pos = first_row + jnp.arange(TOK_DEV, dtype=jnp.int32)
    visible = jnp.arange(TOKENS, dtype=jnp.int32)[None, :] <= row_pos[:, None]
    scores = jnp.where(visible, scores, -1e30)
    top = jnp.max(scores, axis=-1, keepdims=True)
    weights = jnp.exp(scores - top)
    probs = weights / jnp.sum(weights, axis=-1, keepdims=True)
    prob_grad = jnp.einsum("ihgd,jhd->hgij", cotangent, value_rows)
    row_delta = jnp.sum(probs * prob_grad, axis=-1, keepdims=True)
    score_grad = (probs * (prob_grad - row_delta) * inv_scale).astype(jnp.bfloat16)
    probs_low = probs.astype(jnp.bfloat16)
    query_grad = jnp.einsum("hgij,jhd->ihgd", score_grad.astype(jnp.float32), key_rows)
    key_grad = jnp.einsum("hgij,ihgd->jhd", score_grad.astype(jnp.float32), query_heads)
    value_grad = jnp.einsum("hgij,ihgd->jhd", probs_low.astype(jnp.float32), cotangent)
    term = jnp.stack([key_grad, value_grad]).reshape(2, TOKENS, KV_HEADS * HEAD_DIM).astype(jnp.bfloat16)
    term = lax.optimization_barrier(term)
    return query_grad.reshape(TOK_DEV, HEADS * HEAD_DIM).astype(jnp.bfloat16), term.astype(jnp.float32)


def reference(queries, out_grad, kv_codes, kv_scales):
    cache = dequantize(kv_codes, kv_scales)
    total = jnp.zeros((2, TOKENS, KV_HEADS * HEAD_DIM), jnp.float32)
    results = []
    for layer in range(SECTIONS):
        query_blocks = queries[layer].reshape(N_BLK, TOK_DEV, HEADS * HEAD_DIM)
        grad_blocks = out_grad[layer].reshape(N_BLK, TOK_DEV, HEADS * HEAD_DIM)

        def step(carry, item):
            query_rows, cotangent_rows, shard = item
            query_part, term = shard_grads(query_rows, cotangent_rows, cache, shard * TOK_DEV)
            return carry + term, query_part

        total, query_parts = lax.scan(step, total, (query_blocks, grad_blocks, jnp.arange(N_BLK, dtype=jnp.int32)))
        results.append(query_parts.reshape(TOKENS, HEADS * HEAD_DIM))
    return jnp.stack(results), total
```

```python
import functools
import math

import jax
import jax.numpy as jnp
from jax import lax
from jax.experimental import pallas as pl
from jax.experimental.pallas import tpu as pltpu
from jax.sharding import PartitionSpec as P

HEAD_DIM = 128
GROUPS = 4
QUANT_BLOCK = 32
ROWS = 128
BLOCKS = 32
WIDTH = GROUPS * HEAD_DIM
AXES = ("section", "blk")
SCALE = 1.0 / math.sqrt(HEAD_DIM)
EXP2_SCALE = SCALE * math.log2(math.e)
F32 = jnp.float32
BF16 = jnp.bfloat16
NT = (((1,), (1,)), ((), ()))
NN = (((1,), (0,)), ((), ()))

STACK = 2
KEYS = 512
SPAN = KEYS // ROWS
STEP_ROWS = STACK * WIDTH
STEPS = 8 // STACK
CHUNKS = BLOCKS // SPAN
ORDER = (0, 2, 4, 6, 1, 3, 5, 7)


def flip(blk):
    return blk ^ 30


def attention_kernel(blocks_ref, *refs):
    units, kv_ref, outs, term_ref = refs[:8], refs[8], refs[9:17], refs[17]
    q_s, do_s, kt_s, w_s, g_s, m_s, dk_s, dv_s, dq_s = refs[18:]
    for n, k in enumerate(ORDER):
        for g in range(GROUPS):
            lo = (n % STACK) * WIDTH + g * HEAD_DIM
            q_s[n // STACK, lo : lo + ROWS, :] = units[k][0, :, g * HEAD_DIM : (g + 1) * HEAD_DIM]
            do_s[n // STACK, lo : lo + ROWS, :] = units[k][1, :, g * HEAD_DIM : (g + 1) * HEAD_DIM]
    for j in range(BLOCKS):
        kt_s[:, j * ROWS : (j + 1) * ROWS] = kv_ref[j, 0].T
    dk_s[...] = jnp.zeros_like(dk_s)
    dv_s[...] = jnp.zeros_like(dv_s)

    def one_group(group, _):
        block = blocks_ref[group // (STEPS // 2)]
        last = block // SPAN
        q, do = q_s.at[group], do_s.at[group]

        def keys(j, which):
            return kv_ref[pl.ds(j * SPAN, SPAN), which].reshape(KEYS, HEAD_DIM)

        def fold(x, op):
            return op(x.reshape(KEYS // 8, 8, STEP_ROWS), axis=0)

        def forward(j, carry, masked):
            top, total8, dot8 = carry
            scores = lax.dot_general(keys(j, 0), q[...], NT, preferred_element_type=F32)
            if masked:
                key_at = lax.broadcasted_iota(jnp.int32, (KEYS, STEP_ROWS), 0)
                row_at = lax.broadcasted_iota(jnp.int32, (KEYS, STEP_ROWS), 1) & (ROWS - 1)
                scores = jnp.where(key_at <= row_at + (block - j * SPAN) * ROWS, scores, -1e30)
            prob_grad = lax.dot_general(keys(j, 1), do[...], NT, preferred_element_type=F32)
            here = jnp.max(fold(scores, jnp.max), axis=0, keepdims=True) * EXP2_SCALE
            new_top = here if masked else jnp.maximum(top, here)
            weights = jnp.exp2(scores * EXP2_SCALE - new_top)
            w_s[j] = weights
            g_s[j] = prob_grad
            m_s[j] = jnp.broadcast_to(new_top, (8, STEP_ROWS))
            total, dot = fold(weights, jnp.sum), fold(weights * prob_grad, jnp.sum)
            if masked:
                return new_top, total, dot
            factor = jnp.exp2(top - new_top)
            return new_top, total8 * factor + total, dot8 * factor + dot

        start = forward(last, (None, None, None), True)
        top, total8, dot8 = lax.fori_loop(0, last, lambda j, c: forward(j, c, False), start)
        inverse = 1.0 / jnp.sum(total8, axis=0, keepdims=True)
        delta = jnp.sum(dot8, axis=0, keepdims=True) * inverse
        dq_s[...] = jnp.zeros_like(dq_s)

        def backward(j, _):
            factor = jnp.exp2(m_s[j][0:1] - top) * inverse
            probs = w_s[j] * factor
            score_grad = (probs * (g_s[j] - delta)).astype(BF16)
            dv_s[j] += lax.dot_general(probs.astype(BF16), do[...], NN, preferred_element_type=F32)
            dk_s[j] += lax.dot_general(score_grad, q[...], NN, preferred_element_type=F32)
            columns = kt_s[:, pl.ds(pl.multiple_of(j * KEYS, KEYS), KEYS)]
            dq_s[...] += lax.dot_general(columns, score_grad, NN, preferred_element_type=F32)
            return 0

        lax.fori_loop(0, last + 1, backward, 0)
        for h in range(STEP_ROWS // ROWS):
            part = dq_s[:, h * ROWS : (h + 1) * ROWS]
            q_s[group, h * ROWS : (h + 1) * ROWS, :] = (part.T * SCALE).astype(BF16)
        return 0

    lax.fori_loop(0, STEPS, one_group, 0)
    for n, k in enumerate(ORDER):
        for g in range(GROUPS):
            lo = (n % STACK) * WIDTH + g * HEAD_DIM
            outs[k][:, g * HEAD_DIM : (g + 1) * HEAD_DIM] = q_s[n // STACK, lo : lo + ROWS, :]
    for j in range(CHUNKS):
        term_ref[j * SPAN : (j + 1) * SPAN, 0] = (dk_s[j] * SCALE).astype(BF16).reshape(SPAN, ROWS, HEAD_DIM)
        term_ref[j * SPAN : (j + 1) * SPAN, 1] = dv_s[j].astype(BF16).reshape(SPAN, ROWS, HEAD_DIM)


def attention(blocks, units, kv):
    vmem = pl.BlockSpec(memory_space=pltpu.VMEM)
    return pl.pallas_call(
        attention_kernel,
        out_shape=[jax.ShapeDtypeStruct((ROWS, WIDTH), BF16)] * 8
        + [jax.ShapeDtypeStruct((BLOCKS, 2, ROWS, HEAD_DIM), BF16)],
        in_specs=[pl.BlockSpec(memory_space=pltpu.SMEM)] + [vmem] * 9,
        out_specs=[vmem] * 9,
        scratch_shapes=[
            pltpu.VMEM((STEPS, STEP_ROWS, HEAD_DIM), BF16),
            pltpu.VMEM((STEPS, STEP_ROWS, HEAD_DIM), BF16),
            pltpu.VMEM((HEAD_DIM, BLOCKS * ROWS), BF16),
            pltpu.VMEM((CHUNKS, KEYS, STEP_ROWS), F32),
            pltpu.VMEM((CHUNKS, KEYS, STEP_ROWS), F32),
            pltpu.VMEM((CHUNKS, 8, STEP_ROWS), F32),
            pltpu.VMEM((CHUNKS, KEYS, HEAD_DIM), F32),
            pltpu.VMEM((CHUNKS, KEYS, HEAD_DIM), F32),
            pltpu.VMEM((HEAD_DIM, STEP_ROWS), F32),
        ],
        compiler_params=pltpu.CompilerParams(vmem_limit_bytes=60 * 1024 * 1024),
        cost_estimate=pl.CostEstimate(flops=20_000_000_000, bytes_accessed=8_000_000, transcendentals=9_000_000),
        name="attention",
    )(blocks, *units, kv)


def partners(k):
    return [
        (s * BLOCKS + b, (s ^ (k >> 1)) * BLOCKS + (flip(b) if k & 1 else b)) for s in range(4) for b in range(BLOCKS)
    ]


def shards(queries, out_grad, kv_codes, kv_scales):
    section, blk = lax.axis_index("section"), lax.axis_index("blk")
    head = section * 2 + blk // 16

    codes = kv_codes.reshape(2, ROWS // QUANT_BLOCK, QUANT_BLOCK, 2, HEAD_DIM).astype(F32)
    cache = (codes * kv_scales[:, :, None, :, None]).astype(BF16)
    cache = cache.reshape(2, ROWS, 2, HEAD_DIM).transpose(2, 0, 1, 3)
    spread = jnp.broadcast_to(cache[:, None], (2, 16, 2, ROWS, HEAD_DIM)).reshape(BLOCKS, 2, ROWS, HEAD_DIM)

    units = []
    for k in range(8):
        at = (head ^ k) * WIDTH
        unit = jnp.stack(
            [lax.dynamic_slice_in_dim(queries[0], at, WIDTH, 1), lax.dynamic_slice_in_dim(out_grad[0], at, WIDTH, 1)]
        )
        units.append(lax.ppermute(unit, AXES, partners(k)) if k else unit)
    kv = lax.all_to_all(spread, "blk", 0, 0, tiled=True)

    blocks = jnp.stack([blk, flip(blk)]).astype(jnp.int32)
    *grads, term = attention(blocks, units, kv)

    received = lax.all_to_all(term, "blk", 0, 0, tiled=True)
    kv_grad = received.reshape(2, 16, 2, ROWS, HEAD_DIM).astype(F32).sum(1)
    kv_grad = kv_grad.transpose(1, 2, 0, 3).reshape(2, ROWS, 2 * HEAD_DIM)

    query_grad = jnp.zeros((ROWS, 8 * WIDTH), BF16)
    for k in range(8):
        grad = lax.ppermute(grads[k], AXES, partners(k)) if k else grads[k]
        query_grad = lax.dynamic_update_slice_in_dim(query_grad, grad, (head ^ k) * WIDTH, 1)
    return query_grad[None], kv_grad


def solution(mesh):
    in_specs = (
        P("section", "blk", None),
        P("section", "blk", None),
        P(None, "blk", "section"),
        P(None, "blk", "section"),
    )
    out_specs = (P("section", "blk", None), P(None, "blk", "section"))
    return jax.shard_map(shards, mesh=mesh, in_specs=in_specs, out_specs=out_specs, check_vma=False)
```

```python
import functools
import math

import jax
import jax.numpy as jnp
from jax import lax
from jax.experimental import pallas as pl
from jax.experimental.pallas import tpu as pltpu
from jax.sharding import PartitionSpec as P

HEAD_DIM = 128
GROUPS = 4
QUANT_BLOCK = 32
ROWS = 128
BLOCKS = 32
WIDTH = GROUPS * HEAD_DIM
AXES = ("section", "blk")
SCALE = 1.0 / math.sqrt(HEAD_DIM)
EXP2_SCALE = SCALE * math.log2(math.e)
F32 = jnp.float32
BF16 = jnp.bfloat16
NT = (((1,), (1,)), ((), ()))
NN = (((1,), (0,)), ((), ()))

LAYERS = 2
KEYS = 512
SPAN = KEYS // ROWS
GROUP_ROWS = LAYERS * WIDTH
CHUNKS = BLOCKS // SPAN


def flip(blk):
    return blk ^ 30


def attention_kernel(first, blocks_ref, *refs):
    units, kv_ref, refs = (refs[0:2], refs[2:4]), refs[4], refs[5:]
    if not first:
        dk_in, dv_in, refs = refs[0], refs[1], refs[2:]
    outs, refs = refs[:2], refs[2:]
    if first:
        dk_s, dv_s, refs = refs[0], refs[1], refs[2:]
    else:
        term_ref, refs = refs[0], refs[1:]
    q_s, do_s, kt_s, w_s, g_s, m_s, dq_s = refs[:7]
    if not first:
        dk_s, dv_s = refs[7:]
    for n in range(2):
        for layer in range(LAYERS):
            for g in range(GROUPS):
                lo = layer * WIDTH + g * HEAD_DIM
                columns = slice(g * HEAD_DIM, (g + 1) * HEAD_DIM)
                q_s[n, lo : lo + ROWS, :] = units[n][layer][0, 0, :, columns]
                do_s[n, lo : lo + ROWS, :] = units[n][layer][0, 1, :, columns]
    for j in range(BLOCKS):
        kt_s[:, j * ROWS : (j + 1) * ROWS] = kv_ref[j, 0].T
    if first:
        dk_s[...] = jnp.zeros_like(dk_s)
        dv_s[...] = jnp.zeros_like(dv_s)
    else:
        dk_s[...] = dk_in[...]
        dv_s[...] = dv_in[...]

    def one_group(group, _):
        block = blocks_ref[group]
        last = block // SPAN
        q, do = q_s.at[group], do_s.at[group]

        def keys(j, which):
            return kv_ref[pl.ds(j * SPAN, SPAN), which].reshape(KEYS, HEAD_DIM)

        def fold(x, op):
            return op(x.reshape(KEYS // 8, 8, GROUP_ROWS), axis=0)

        def forward(j, carry, masked):
            top, total8, dot8 = carry
            scores = lax.dot_general(keys(j, 0), q[...], NT, preferred_element_type=F32)
            if masked:
                key_at = lax.broadcasted_iota(jnp.int32, (KEYS, GROUP_ROWS), 0)
                row_at = lax.broadcasted_iota(jnp.int32, (KEYS, GROUP_ROWS), 1) & (ROWS - 1)
                scores = jnp.where(key_at <= row_at + (block - j * SPAN) * ROWS, scores, -1e30)
            prob_grad = lax.dot_general(keys(j, 1), do[...], NT, preferred_element_type=F32)
            here = jnp.max(fold(scores, jnp.max), axis=0, keepdims=True) * EXP2_SCALE
            new_top = here if masked else jnp.maximum(top, here)
            weights = jnp.exp2(scores * EXP2_SCALE - new_top)
            w_s[j] = weights
            g_s[j] = prob_grad
            m_s[j] = jnp.broadcast_to(new_top, (8, GROUP_ROWS))
            total, dot = fold(weights, jnp.sum), fold(weights * prob_grad, jnp.sum)
            if masked:
                return new_top, total, dot
            factor = jnp.exp2(top - new_top)
            return new_top, total8 * factor + total, dot8 * factor + dot

        start = forward(last, (None, None, None), True)
        top, total8, dot8 = lax.fori_loop(0, last, lambda j, c: forward(j, c, False), start)
        inverse = 1.0 / jnp.sum(total8, axis=0, keepdims=True)
        delta = jnp.sum(dot8, axis=0, keepdims=True) * inverse
        dq_s[...] = jnp.zeros_like(dq_s)

        def backward(j, _):
            factor = jnp.exp2(m_s[j][0:1] - top) * inverse
            probs = w_s[j] * factor
            score_grad = (probs * (g_s[j] - delta)).astype(BF16)
            dv_s[j] += lax.dot_general(probs.astype(BF16), do[...], NN, preferred_element_type=F32)
            dk_s[j] += lax.dot_general(score_grad, q[...], NN, preferred_element_type=F32)
            columns = kt_s[:, pl.ds(pl.multiple_of(j * KEYS, KEYS), KEYS)]
            dq_s[...] += lax.dot_general(columns, score_grad, NN, preferred_element_type=F32)
            return 0

        lax.fori_loop(0, last + 1, backward, 0)
        for h in range(GROUP_ROWS // ROWS):
            part = dq_s[:, h * ROWS : (h + 1) * ROWS]
            q_s[group, h * ROWS : (h + 1) * ROWS, :] = (part.T * SCALE).astype(BF16)
        return 0

    lax.fori_loop(0, 2, one_group, 0)
    for n in range(2):
        for layer in range(LAYERS):
            for g in range(GROUPS):
                lo = layer * WIDTH + g * HEAD_DIM
                outs[n][layer, :, g * HEAD_DIM : (g + 1) * HEAD_DIM] = q_s[n, lo : lo + ROWS, :]
    if not first:
        for j in range(CHUNKS):
            blocks = slice(j * SPAN, (j + 1) * SPAN)
            term_ref[blocks, 0] = (dk_s[j] * SCALE).astype(BF16).reshape(SPAN, ROWS, HEAD_DIM)
            term_ref[blocks, 1] = dv_s[j].astype(BF16).reshape(SPAN, ROWS, HEAD_DIM)


def attention(blocks, units, kv, sums=None):
    first = sums is None
    vmem = pl.BlockSpec(memory_space=pltpu.VMEM)
    total = (CHUNKS, KEYS, HEAD_DIM)
    grads = [jax.ShapeDtypeStruct((LAYERS, ROWS, WIDTH), BF16)] * 2
    scratch = [
        pltpu.VMEM((2, GROUP_ROWS, HEAD_DIM), BF16),
        pltpu.VMEM((2, GROUP_ROWS, HEAD_DIM), BF16),
        pltpu.VMEM((HEAD_DIM, BLOCKS * ROWS), BF16),
        pltpu.VMEM((CHUNKS, KEYS, GROUP_ROWS), F32),
        pltpu.VMEM((CHUNKS, KEYS, GROUP_ROWS), F32),
        pltpu.VMEM((CHUNKS, 8, GROUP_ROWS), F32),
        pltpu.VMEM((HEAD_DIM, GROUP_ROWS), F32),
    ]
    if first:
        outs = grads + [jax.ShapeDtypeStruct(total, F32)] * 2
    else:
        outs = grads + [jax.ShapeDtypeStruct((BLOCKS, 2, ROWS, HEAD_DIM), BF16)]
        scratch += [pltpu.VMEM(total, F32)] * 2
    args = [*units[0], *units[1], kv] + ([] if first else list(sums))
    return pl.pallas_call(
        functools.partial(attention_kernel, first),
        out_shape=outs,
        in_specs=[pl.BlockSpec(memory_space=pltpu.SMEM)] + [vmem] * len(args),
        out_specs=[vmem] * len(outs),
        scratch_shapes=scratch,
        compiler_params=pltpu.CompilerParams(vmem_limit_bytes=60 * 1024 * 1024),
        cost_estimate=pl.CostEstimate(flops=12_000_000_000, bytes_accessed=8_000_000, transcendentals=4_500_000),
        name="attention_first" if first else "attention_second",
    )(blocks, *args)


CORE, FLIP, NEAR = 1, 2, 4


def partners(k):
    return [
        (s * BLOCKS + b, (s ^ (k & CORE) ^ (2 if k & NEAR else 0)) * BLOCKS + (flip(b) if k & FLIP else b))
        for s in range(4)
        for b in range(BLOCKS)
    ]


def move(x, k):
    return lax.ppermute(x, AXES, partners(k)) if k else x


def shards(queries, out_grad, kv_codes, kv_scales):
    section, blk = lax.axis_index("section"), lax.axis_index("blk")
    head = section * 2 + blk // 16

    def of(k):
        return head ^ (4 if k & NEAR else 0) ^ (2 if k & CORE else 0) ^ (1 if k & FLIP else 0)

    codes = kv_codes.reshape(2, ROWS // QUANT_BLOCK, QUANT_BLOCK, 2, HEAD_DIM).astype(F32)
    cache = (codes * kv_scales[:, :, None, :, None]).astype(BF16)
    cache = cache.reshape(2, ROWS, 2, HEAD_DIM).transpose(2, 0, 1, 3)
    spread = jnp.broadcast_to(cache[:, None], (2, 16, 2, ROWS, HEAD_DIM)).reshape(BLOCKS, 2, ROWS, HEAD_DIM)
    kv = lax.all_to_all(spread, "blk", 0, 0, tiled=True)

    def pick(k):
        at = of(k) * WIDTH
        return [lax.dynamic_slice_in_dim(queries[0], at, WIDTH, 1), lax.dynamic_slice_in_dim(out_grad[0], at, WIDTH, 1)]

    def packed(k):
        return jnp.stack(pick(k) + pick(k | CORE)).reshape(2, 2, ROWS, WIDTH)

    def fetch(x):
        return (x, move(x[1:], CORE))

    def give(x):
        return (x[0], move(x[1], CORE))

    blocks = jnp.stack([blk, flip(blk)]).astype(jnp.int32)
    own = packed(0)
    turned = move(packed(FLIP), FLIP)
    near, near_turned, kv = lax.optimization_barrier((packed(NEAR), packed(NEAR | FLIP), kv))
    near = move(near, NEAR)
    near_turned = move(near_turned, NEAR | FLIP)
    d_own, d_turned, *sums = attention(blocks, (fetch(own), fetch(turned)), kv)
    d_near, d_near_turned, term = attention(blocks, (fetch(near), fetch(near_turned)), kv, sums)

    received = lax.all_to_all(term, "blk", 0, 0, tiled=True)
    kv_grad = received.reshape(2, 16, 2, ROWS, HEAD_DIM).astype(F32).sum(1)
    kv_grad = kv_grad.transpose(1, 2, 0, 3).reshape(2, ROWS, 2 * HEAD_DIM)

    query_grad = jnp.zeros((ROWS, 8 * WIDTH), BF16)
    for k, grad in ((0, d_own), (FLIP, d_turned), (NEAR, d_near), (NEAR | FLIP, d_near_turned)):
        for c, part in enumerate(give(move(grad, k))):
            query_grad = lax.dynamic_update_slice_in_dim(query_grad, part, of(k | c) * WIDTH, 1)
    return query_grad[None], kv_grad


def solution(mesh):
    in_specs = (
        P("section", "blk", None),
        P("section", "blk", None),
        P(None, "blk", "section"),
        P(None, "blk", "section"),
    )
    out_specs = (P("section", "blk", None), P(None, "blk", "section"))
    return jax.shard_map(shards, mesh=mesh, in_specs=in_specs, out_specs=out_specs, check_vma=False)
```

```python
import functools
import math

import jax
import jax.numpy as jnp
from jax import lax
from jax.experimental import pallas as pl
from jax.experimental.pallas import tpu as pltpu
from jax.sharding import PartitionSpec as P

HEAD_DIM = 128
GROUPS = 4
QUANT_BLOCK = 32
ROWS = 128
BLOCKS = 32
WIDTH = GROUPS * HEAD_DIM
AXES = ("section", "blk")
SCALE = 1.0 / math.sqrt(HEAD_DIM)
EXP2_SCALE = SCALE * math.log2(math.e)
F32 = jnp.float32
BF16 = jnp.bfloat16
NT = (((1,), (1,)), ((), ()))
NN = (((1,), (0,)), ((), ()))

LAYERS = 2
KEYS = 512
SPAN = KEYS // ROWS
GROUP_ROWS = LAYERS * WIDTH
CHUNKS = BLOCKS // SPAN


def flip(blk):
    return blk ^ 30


def attention_kernel(first, blocks_ref, *refs):
    units, kv_ref, refs = (refs[0:2], refs[2:4]), refs[4], refs[5:]
    if not first:
        dk_in, dv_in, refs = refs[0], refs[1], refs[2:]
    outs, refs = refs[:2], refs[2:]
    if first:
        dk_s, dv_s, refs = refs[0], refs[1], refs[2:]
    else:
        term_ref, refs = refs[0], refs[1:]
    q_s, do_s, kt_s, w_s, g_s, m_s, dq_s = refs[:7]
    if not first:
        dk_s, dv_s = refs[7:]
    for n in range(2):
        for layer in range(LAYERS):
            for g in range(GROUPS):
                lo = layer * WIDTH + g * HEAD_DIM
                columns = slice(g * HEAD_DIM, (g + 1) * HEAD_DIM)
                q_s[n, lo : lo + ROWS, :] = units[n][layer][0, 0, :, columns]
                do_s[n, lo : lo + ROWS, :] = units[n][layer][0, 1, :, columns]
    for j in range(BLOCKS):
        kt_s[:, j * ROWS : (j + 1) * ROWS] = kv_ref[j, 0].T
    if first:
        dk_s[...] = jnp.zeros_like(dk_s)
        dv_s[...] = jnp.zeros_like(dv_s)
    else:
        dk_s[...] = dk_in[...]
        dv_s[...] = dv_in[...]

    def one_group(group, _):
        block = blocks_ref[group]
        last = block // SPAN
        q, do = q_s.at[group], do_s.at[group]

        def keys(j, which):
            return kv_ref[pl.ds(j * SPAN, SPAN), which].reshape(KEYS, HEAD_DIM)

        def fold(x, op):
            return op(x.reshape(KEYS // 8, 8, GROUP_ROWS), axis=0)

        def forward(j, carry, masked):
            top, total8, dot8 = carry
            scores = lax.dot_general(keys(j, 0), q[...], NT, preferred_element_type=F32)
            if masked:
                key_at = lax.broadcasted_iota(jnp.int32, (KEYS, GROUP_ROWS), 0)
                row_at = lax.broadcasted_iota(jnp.int32, (KEYS, GROUP_ROWS), 1) & (ROWS - 1)
                scores = jnp.where(key_at <= row_at + (block - j * SPAN) * ROWS, scores, -1e30)
            prob_grad = lax.dot_general(keys(j, 1), do[...], NT, preferred_element_type=F32)
            here = jnp.max(fold(scores, jnp.max), axis=0, keepdims=True) * EXP2_SCALE
            new_top = here if masked else jnp.maximum(top, here)
            weights = jnp.exp2(scores * EXP2_SCALE - new_top)
            w_s[j] = weights
            g_s[j] = prob_grad
            m_s[j] = jnp.broadcast_to(new_top, (8, GROUP_ROWS))
            total, dot = fold(weights, jnp.sum), fold(weights * prob_grad, jnp.sum)
            if masked:
                return new_top, total, dot
            factor = jnp.exp2(top - new_top)
            return new_top, total8 * factor + total, dot8 * factor + dot

        start = forward(last, (None, None, None), True)
        top, total8, dot8 = lax.fori_loop(0, last, lambda j, c: forward(j, c, False), start)
        inverse = 1.0 / jnp.sum(total8, axis=0, keepdims=True)
        delta = jnp.sum(dot8, axis=0, keepdims=True) * inverse
        dq_s[...] = jnp.zeros_like(dq_s)

        def backward(j, _):
            factor = jnp.exp2(m_s[j][0:1] - top) * inverse
            probs = w_s[j] * factor
            score_grad = (probs * (g_s[j] - delta)).astype(BF16)
            dv_s[j] += lax.dot_general(probs.astype(BF16), do[...], NN, preferred_element_type=F32)
            dk_s[j] += lax.dot_general(score_grad, q[...], NN, preferred_element_type=F32)
            columns = kt_s[:, pl.ds(pl.multiple_of(j * KEYS, KEYS), KEYS)]
            dq_s[...] += lax.dot_general(columns, score_grad, NN, preferred_element_type=F32)
            return 0

        lax.fori_loop(0, last + 1, backward, 0)
        for h in range(GROUP_ROWS // ROWS):
            part = dq_s[:, h * ROWS : (h + 1) * ROWS]
            q_s[group, h * ROWS : (h + 1) * ROWS, :] = (part.T * SCALE).astype(BF16)
        return 0

    lax.fori_loop(0, 2, one_group, 0)
    for n in range(2):
        for layer in range(LAYERS):
            for g in range(GROUPS):
                lo = layer * WIDTH + g * HEAD_DIM
                outs[n][layer, :, g * HEAD_DIM : (g + 1) * HEAD_DIM] = q_s[n, lo : lo + ROWS, :]
    if not first:
        for j in range(CHUNKS):
            blocks = slice(j * SPAN, (j + 1) * SPAN)
            term_ref[blocks, 0] = (dk_s[j] * SCALE).astype(BF16).reshape(SPAN, ROWS, HEAD_DIM)
            term_ref[blocks, 1] = dv_s[j].astype(BF16).reshape(SPAN, ROWS, HEAD_DIM)


def attention(blocks, units, kv, sums=None):
    first = sums is None
    vmem = pl.BlockSpec(memory_space=pltpu.VMEM)
    total = (CHUNKS, KEYS, HEAD_DIM)
    grads = [jax.ShapeDtypeStruct((LAYERS, ROWS, WIDTH), BF16)] * 2
    scratch = [
        pltpu.VMEM((2, GROUP_ROWS, HEAD_DIM), BF16),
        pltpu.VMEM((2, GROUP_ROWS, HEAD_DIM), BF16),
        pltpu.VMEM((HEAD_DIM, BLOCKS * ROWS), BF16),
        pltpu.VMEM((CHUNKS, KEYS, GROUP_ROWS), F32),
        pltpu.VMEM((CHUNKS, KEYS, GROUP_ROWS), F32),
        pltpu.VMEM((CHUNKS, 8, GROUP_ROWS), F32),
        pltpu.VMEM((HEAD_DIM, GROUP_ROWS), F32),
    ]
    if first:
        outs = grads + [jax.ShapeDtypeStruct(total, F32)] * 2
    else:
        outs = grads + [jax.ShapeDtypeStruct((BLOCKS, 2, ROWS, HEAD_DIM), BF16)]
        scratch += [pltpu.VMEM(total, F32)] * 2
    args = [*units[0], *units[1], kv] + ([] if first else list(sums))
    return pl.pallas_call(
        functools.partial(attention_kernel, first),
        out_shape=outs,
        in_specs=[pl.BlockSpec(memory_space=pltpu.SMEM)] + [vmem] * len(args),
        out_specs=[vmem] * len(outs),
        scratch_shapes=scratch,
        compiler_params=pltpu.CompilerParams(vmem_limit_bytes=60 * 1024 * 1024),
        cost_estimate=pl.CostEstimate(flops=12_000_000_000, bytes_accessed=8_000_000, transcendentals=4_500_000),
        name="attention_first" if first else "attention_second",
    )(blocks, *args)


CORE, FLIP, NEAR = 1, 2, 4


def partners(k):
    return [
        (s * BLOCKS + b, (s ^ (k & CORE) ^ (2 if k & NEAR else 0)) * BLOCKS + (flip(b) if k & FLIP else b))
        for s in range(4)
        for b in range(BLOCKS)
    ]


def move(x, k):
    return lax.ppermute(x, AXES, partners(k)) if k else x


def shards(queries, out_grad, kv_codes, kv_scales):
    section, blk = lax.axis_index("section"), lax.axis_index("blk")
    head = section * 2 + blk // 16

    def of(k):
        return head ^ (4 if k & NEAR else 0) ^ (2 if k & CORE else 0) ^ (1 if k & FLIP else 0)

    codes = kv_codes.reshape(2, ROWS // QUANT_BLOCK, QUANT_BLOCK, 2, HEAD_DIM).astype(F32)
    cache = (codes * kv_scales[:, :, None, :, None]).astype(BF16)
    cache = cache.reshape(2, ROWS, 2, HEAD_DIM).transpose(2, 0, 1, 3)
    spread = jnp.broadcast_to(cache[:, None], (2, 16, 2, ROWS, HEAD_DIM)).reshape(BLOCKS, 2, ROWS, HEAD_DIM)
    kv = lax.all_to_all(spread, "blk", 0, 0, tiled=True)

    def pick(k):
        at = of(k) * WIDTH
        return [lax.dynamic_slice_in_dim(queries[0], at, WIDTH, 1), lax.dynamic_slice_in_dim(out_grad[0], at, WIDTH, 1)]

    def packed(k):
        return jnp.stack(pick(k) + pick(k | CORE)).reshape(2, 2, ROWS, WIDTH)

    def fetch(x):
        return (x, move(x[1:], CORE))

    def give(x):
        return (x[0], move(x[1], CORE))

    blocks = jnp.stack([blk, flip(blk)]).astype(jnp.int32)
    own = packed(0)
    across = move(packed(NEAR | FLIP), NEAR | FLIP)
    near, turned, kv = lax.optimization_barrier((packed(NEAR), packed(FLIP), kv))
    near, turned = move(near, NEAR), move(turned, FLIP)
    d_own, d_across, *sums = attention(blocks, (fetch(own), fetch(across)), kv)
    near, turned, sums = lax.optimization_barrier((near, turned, sums))
    d_near, d_turned, term = attention(blocks, (fetch(near), fetch(turned)), kv, sums)

    received = lax.all_to_all(term, "blk", 0, 0, tiled=True)
    kv_grad = received.reshape(2, 16, 2, ROWS, HEAD_DIM).astype(F32).sum(1)
    kv_grad = kv_grad.transpose(1, 2, 0, 3).reshape(2, ROWS, 2 * HEAD_DIM)

    query_grad = jnp.zeros((ROWS, 8 * WIDTH), BF16)
    for k, grad in ((0, d_own), (NEAR | FLIP, d_across), (NEAR, d_near), (FLIP, d_turned)):
        for c, part in enumerate(give(move(grad, k))):
            query_grad = lax.dynamic_update_slice_in_dim(query_grad, part, of(k | c) * WIDTH, 1)
    return query_grad[None], kv_grad


def solution(mesh):
    in_specs = (
        P("section", "blk", None),
        P("section", "blk", None),
        P(None, "blk", "section"),
        P(None, "blk", "section"),
    )
    out_specs = (P("section", "blk", None), P(None, "blk", "section"))
    return jax.shard_map(shards, mesh=mesh, in_specs=in_specs, out_specs=out_specs, check_vma=False)
```

```python
import functools
import math

import jax
import jax.numpy as jnp
from jax import lax
from jax.experimental import pallas as pl
from jax.experimental.pallas import tpu as pltpu
from jax.sharding import PartitionSpec as P

HEAD_DIM = 128
GROUPS = 4
QUANT_BLOCK = 32
ROWS = 128
BLOCKS = 32
WIDTH = GROUPS * HEAD_DIM
AXES = ("section", "blk")
SCALE = 1.0 / math.sqrt(HEAD_DIM)
EXP2_SCALE = SCALE * math.log2(math.e)
F32 = jnp.float32
BF16 = jnp.bfloat16
NT = (((1,), (1,)), ((), ()))
NN = (((1,), (0,)), ((), ()))

LAYERS = 2
KEYS = 256
UNROLL = 4
SPAN = KEYS // ROWS
GROUP_ROWS = LAYERS * WIDTH
CHUNKS = BLOCKS // SPAN
HEADROOM = 64.0


def flip(blk):
    return blk ^ 30


def attention_kernel(first, blocks_ref, *refs):
    units, refs = refs[:4], refs[4:]
    kv_ref, refs = refs[0], refs[1:]
    if not first:
        sums_ref, refs = refs[0], refs[1:]
    mine_ref, other_ref, term_ref = refs[:3]
    q_s, do_s, kt_s, w_s, g_s, m_s, dk_s, dv_s, dq_s, stat_s = refs[3:]
    for n in range(2):
        for layer in range(LAYERS):
            unit = units[n * LAYERS + layer]
            for g in range(GROUPS):
                lo = layer * WIDTH + g * HEAD_DIM
                columns = slice(g * HEAD_DIM, (g + 1) * HEAD_DIM)
                q_s[n, lo : lo + ROWS, :] = unit[0, :, columns]
                do_s[n, lo : lo + ROWS, :] = unit[1, :, columns]
    for j in range(BLOCKS):
        kt_s[:, j * ROWS : (j + 1) * ROWS] = kv_ref[j, 0].T
    if first:
        dk_s[...] = jnp.zeros_like(dk_s)
        dv_s[...] = jnp.zeros_like(dv_s)
    else:
        for j in range(CHUNKS):
            blocks = slice(j * SPAN, (j + 1) * SPAN)
            dk_s[j] = sums_ref[blocks, 0].reshape(KEYS, HEAD_DIM).astype(F32)
            dv_s[j] = sums_ref[blocks, 1].reshape(KEYS, HEAD_DIM).astype(F32)

    def one_group(group, _):
        block = blocks_ref[group]
        last = block // SPAN
        q, do = q_s.at[group], do_s.at[group]

        def keys(j, which):
            return kv_ref[pl.ds(j * SPAN, SPAN), which].reshape(KEYS, HEAD_DIM)

        def fold(x, op):
            return op(x.reshape(KEYS // 8, 8, GROUP_ROWS), axis=0)

        def products(j):
            scores = lax.dot_general(keys(j, 0), q[...], NT, preferred_element_type=F32)
            return scores, lax.dot_general(keys(j, 1), do[...], NT, preferred_element_type=F32)

        def keep(j, weights, prob_grad, top):
            w_s[j] = weights
            g_s[j] = prob_grad
            m_s[j] = jnp.broadcast_to(top, (8, GROUP_ROWS))
            return fold(weights, jnp.sum), fold(weights * prob_grad, jnp.sum)

        def highest(scores):
            return jnp.max(fold(scores, jnp.max), axis=0, keepdims=True) * EXP2_SCALE

        def unrolled(count, step, carry):
            def several(t, carry):
                for n in range(UNROLL):
                    carry = step(t * UNROLL + n, carry)
                return carry

            carry = lax.fori_loop(0, count // UNROLL, several, carry)
            return lax.fori_loop(count // UNROLL * UNROLL, count, step, carry)

        scores, prob_grad = products(last)
        key_at = lax.broadcasted_iota(jnp.int32, (KEYS, GROUP_ROWS), 0)
        row_at = lax.broadcasted_iota(jnp.int32, (KEYS, GROUP_ROWS), 1) & (ROWS - 1)
        scores = jnp.where(key_at <= row_at + (block - last * SPAN) * ROWS, scores, -1e30)
        base = highest(scores)
        total0, dot0 = keep(last, jnp.exp2(scores * EXP2_SCALE - base), prob_grad, base)

        def quick(j, carry):
            peak8, total8, dot8 = carry
            scores, prob_grad = products(j)
            total, dot = keep(j, jnp.exp2(scores * EXP2_SCALE - base), prob_grad, base)
            return jnp.maximum(peak8, fold(scores, jnp.max)), total8 + total, dot8 + dot

        peak8, total8, dot8 = unrolled(last, quick, (jnp.full((8, GROUP_ROWS), -1e30, F32), total0, dot0))
        stat_s[0:1] = base
        stat_s[8:16] = total8
        stat_s[16:24] = dot8

        @pl.when(jnp.max(peak8 * EXP2_SCALE - base) > HEADROOM)
        def _():
            def careful(j, carry):
                top, total8, dot8 = carry
                scores, prob_grad = products(j)
                new_top = jnp.maximum(top, highest(scores))
                total, dot = keep(j, jnp.exp2(scores * EXP2_SCALE - new_top), prob_grad, new_top)
                factor = jnp.exp2(top - new_top)
                return new_top, total8 * factor + total, dot8 * factor + dot

            top, total8, dot8 = lax.fori_loop(0, last, careful, (base, total0, dot0))
            stat_s[0:1] = top
            stat_s[8:16] = total8
            stat_s[16:24] = dot8

        top = stat_s[0:1]
        inverse = 1.0 / jnp.sum(stat_s[8:16], axis=0, keepdims=True)
        delta = jnp.sum(stat_s[16:24], axis=0, keepdims=True) * inverse
        dq_s[...] = jnp.zeros_like(dq_s)

        def backward(j, carry):
            probs = w_s[j] * (jnp.exp2(m_s[j][0:1] - top) * inverse)
            score_grad = (probs * (g_s[j] - delta)).astype(BF16)
            dv_s[j] += lax.dot_general(probs.astype(BF16), do[...], NN, preferred_element_type=F32)
            dk_s[j] += lax.dot_general(score_grad, q[...], NN, preferred_element_type=F32)
            columns = kt_s[:, pl.ds(pl.multiple_of(j * KEYS, KEYS), KEYS)]
            dq_s[...] += lax.dot_general(columns, score_grad, NN, preferred_element_type=F32)
            return carry

        unrolled(last + 1, backward, 0)
        for h in range(GROUP_ROWS // ROWS):
            part = dq_s[:, h * ROWS : (h + 1) * ROWS]
            q_s[group, h * ROWS : (h + 1) * ROWS, :] = (part.T * SCALE).astype(BF16)
        return 0

    lax.fori_loop(0, 2, one_group, 0)
    for n in range(2):
        for layer, out_ref in enumerate((mine_ref, other_ref)):
            for g in range(GROUPS):
                lo = layer * WIDTH + g * HEAD_DIM
                out_ref[n, :, g * HEAD_DIM : (g + 1) * HEAD_DIM] = q_s[n, lo : lo + ROWS, :]
    for j in range(CHUNKS):
        blocks = slice(j * SPAN, (j + 1) * SPAN)
        key_grad = dk_s[j] if first else dk_s[j] * SCALE
        term_ref[blocks, 0] = key_grad.astype(BF16).reshape(SPAN, ROWS, HEAD_DIM)
        term_ref[blocks, 1] = dv_s[j].astype(BF16).reshape(SPAN, ROWS, HEAD_DIM)


def attention(blocks, units, kv, sums=None):
    first = sums is None
    vmem = pl.BlockSpec(memory_space=pltpu.VMEM)
    args = [*units, kv] + ([] if first else [sums])
    return pl.pallas_call(
        functools.partial(attention_kernel, first),
        out_shape=[jax.ShapeDtypeStruct((2, ROWS, WIDTH), BF16)] * 2
        + [jax.ShapeDtypeStruct((BLOCKS, 2, ROWS, HEAD_DIM), BF16)],
        in_specs=[pl.BlockSpec(memory_space=pltpu.SMEM)] + [vmem] * len(args),
        out_specs=[vmem] * 3,
        scratch_shapes=[
            pltpu.VMEM((2, GROUP_ROWS, HEAD_DIM), BF16),
            pltpu.VMEM((2, GROUP_ROWS, HEAD_DIM), BF16),
            pltpu.VMEM((HEAD_DIM, BLOCKS * ROWS), BF16),
            pltpu.VMEM((CHUNKS, KEYS, GROUP_ROWS), F32),
            pltpu.VMEM((CHUNKS, KEYS, GROUP_ROWS), F32),
            pltpu.VMEM((CHUNKS, 8, GROUP_ROWS), F32),
            pltpu.VMEM((CHUNKS, KEYS, HEAD_DIM), F32),
            pltpu.VMEM((CHUNKS, KEYS, HEAD_DIM), F32),
            pltpu.VMEM((HEAD_DIM, GROUP_ROWS), F32),
            pltpu.VMEM((24, GROUP_ROWS), F32),
        ],
        compiler_params=pltpu.CompilerParams(vmem_limit_bytes=60 * 1024 * 1024),
        cost_estimate=pl.CostEstimate(flops=12_000_000_000, bytes_accessed=8_000_000, transcendentals=4_500_000),
        name="attention_first" if first else "attention_second",
    )(blocks, *args)


CORE, FLIP, NEAR = 1, 2, 4
ACROSS = NEAR | FLIP


def partners(k):
    return [
        (s * BLOCKS + b, (s ^ (k & CORE) ^ (2 if k & NEAR else 0)) * BLOCKS + (flip(b) if k & FLIP else b))
        for s in range(4)
        for b in range(BLOCKS)
    ]


def move(x, k):
    return lax.ppermute(x, AXES, partners(k))


def shards(queries, out_grad, kv_codes, kv_scales):
    section, blk = lax.axis_index("section"), lax.axis_index("blk")
    head = section * 2 + blk // 16

    def of(k):
        return head ^ (4 if k & NEAR else 0) ^ (2 if k & CORE else 0) ^ (1 if k & FLIP else 0)

    codes = kv_codes.reshape(2, ROWS // QUANT_BLOCK, QUANT_BLOCK, 2, HEAD_DIM).astype(F32)
    cache = (codes * kv_scales[:, :, None, :, None]).astype(BF16)
    cache = cache.reshape(2, ROWS, 2, HEAD_DIM).transpose(2, 0, 1, 3)
    spread = jnp.broadcast_to(cache[:, None], (2, 16, 2, ROWS, HEAD_DIM)).reshape(BLOCKS, 2, ROWS, HEAD_DIM)
    kv = lax.all_to_all(spread, "blk", 0, 0, tiled=True)

    def pick(k):
        at = of(k) * WIDTH
        return jnp.stack(
            [lax.dynamic_slice_in_dim(queries[0], at, WIDTH, 1), lax.dynamic_slice_in_dim(out_grad[0], at, WIDTH, 1)]
        )

    blocks = jnp.stack([blk, flip(blk)]).astype(jnp.int32)
    across = move(pick(ACROSS), ACROSS)
    across_core = move(pick(ACROSS | CORE), ACROSS | CORE)
    own, own_core = pick(0), move(pick(CORE), CORE)
    swapped = move(jnp.stack([pick(NEAR | CORE), pick(FLIP | CORE)]), CORE)
    near, turned, kv = lax.optimization_barrier(
        (jnp.stack([pick(NEAR), swapped[0]]), jnp.stack([pick(FLIP), swapped[1]]), kv)
    )
    near, turned = move(near, NEAR), move(turned, FLIP)

    mine, other, sums = attention(blocks, (own, own_core, across, across_core), kv)
    near, turned, mine = lax.optimization_barrier((near, turned, mine))
    other = move(other, CORE)
    grads = {0: mine[0], CORE: other[0]}
    sent = move(jnp.stack([mine[1], other[1]]), ACROSS)
    grads |= {ACROSS: sent[0], ACROSS | CORE: sent[1]}

    mine, other, term = attention(blocks, (near[0], near[1], turned[0], turned[1]), kv, sums)
    other, term = lax.optimization_barrier((move(other, CORE), term))
    received = lax.all_to_all(term, "blk", 0, 0, tiled=True)
    for n, k in enumerate((NEAR, FLIP)):
        sent = move(jnp.stack([mine[n], other[n]]), k)
        grads |= {k: sent[0], k | CORE: sent[1]}

    kv_grad = received.reshape(2, 16, 2, ROWS, HEAD_DIM).astype(F32).sum(1)
    kv_grad = kv_grad.transpose(1, 2, 0, 3).reshape(2, ROWS, 2 * HEAD_DIM)
    query_grad = jnp.zeros((ROWS, 8 * WIDTH), BF16)
    for k, part in grads.items():
        query_grad = lax.dynamic_update_slice_in_dim(query_grad, part, of(k) * WIDTH, 1)
    return query_grad[None], kv_grad


def solution(mesh):
    in_specs = (
        P("section", "blk", None),
        P("section", "blk", None),
        P(None, "blk", "section"),
        P(None, "blk", "section"),
    )
    out_specs = (P("section", "blk", None), P(None, "blk", "section"))
    return jax.shard_map(shards, mesh=mesh, in_specs=in_specs, out_specs=out_specs, check_vma=False)
```

```python
import functools
import math

import jax
import jax.numpy as jnp
from jax import lax
from jax.experimental import pallas as pl
from jax.experimental.pallas import tpu as pltpu
from jax.sharding import PartitionSpec as P

HEAD_DIM = 128
GROUPS = 4
QUANT_BLOCK = 32
ROWS = 128
BLOCKS = 32
WIDTH = GROUPS * HEAD_DIM
AXES = ("section", "blk")
SCALE = 1.0 / math.sqrt(HEAD_DIM)
EXP2_SCALE = SCALE * math.log2(math.e)
F32 = jnp.float32
BF16 = jnp.bfloat16
NT = (((1,), (1,)), ((), ()))
NN = (((1,), (0,)), ((), ()))

LAYERS = 2
KEYS = 256
UNROLL = 4
SPAN = KEYS // ROWS
GROUP_ROWS = LAYERS * WIDTH
CHUNKS = BLOCKS // SPAN
HEADROOM = 64.0


def flip(blk):
    return blk ^ 30


def attention_kernel(first, blocks_ref, *refs):
    if first:
        units, refs = refs[:4], refs[4:]
    else:
        units, refs = [ref.at[layer] for ref in refs[:2] for layer in range(LAYERS)], refs[2:]
    kv_ref, refs = refs[0], refs[1:]
    if not first:
        sums_ref, refs = refs[0], refs[1:]
    grad_refs, term_ref = refs[:4], refs[4]
    q_s, do_s, kt_s, w_s, g_s, m_s, dk_s, dv_s, dq_s, stat_s = refs[5:]
    for n in range(2):
        for layer in range(LAYERS):
            unit = units[n * LAYERS + layer]
            for g in range(GROUPS):
                lo = layer * WIDTH + g * HEAD_DIM
                columns = slice(g * HEAD_DIM, (g + 1) * HEAD_DIM)
                q_s[n, lo : lo + ROWS, :] = unit[0, :, columns]
                do_s[n, lo : lo + ROWS, :] = unit[1, :, columns]
    for j in range(BLOCKS):
        kt_s[:, j * ROWS : (j + 1) * ROWS] = kv_ref[j, 0].T
    if first:
        dk_s[...] = jnp.zeros_like(dk_s)
        dv_s[...] = jnp.zeros_like(dv_s)
    else:
        for j in range(CHUNKS):
            blocks = slice(j * SPAN, (j + 1) * SPAN)
            dk_s[j] = sums_ref[blocks, 0].reshape(KEYS, HEAD_DIM).astype(F32)
            dv_s[j] = sums_ref[blocks, 1].reshape(KEYS, HEAD_DIM).astype(F32)

    def one_group(group, _):
        block = blocks_ref[group]
        last = block // SPAN
        q, do = q_s.at[group], do_s.at[group]

        def keys(j, which):
            return kv_ref[pl.ds(j * SPAN, SPAN), which].reshape(KEYS, HEAD_DIM)

        def fold(x, op):
            return op(x.reshape(KEYS // 8, 8, GROUP_ROWS), axis=0)

        def products(j):
            scores = lax.dot_general(keys(j, 0), q[...], NT, preferred_element_type=F32)
            return scores, lax.dot_general(keys(j, 1), do[...], NT, preferred_element_type=F32)

        def keep(j, weights, prob_grad, top):
            w_s[j] = weights
            g_s[j] = prob_grad
            m_s[j] = jnp.broadcast_to(top, (8, GROUP_ROWS))
            return fold(weights, jnp.sum), fold(weights * prob_grad, jnp.sum)

        def highest(scores):
            return jnp.max(fold(scores, jnp.max), axis=0, keepdims=True) * EXP2_SCALE

        def unrolled(count, step, carry):
            def several(t, carry):
                for n in range(UNROLL):
                    carry = step(t * UNROLL + n, carry)
                return carry

            carry = lax.fori_loop(0, count // UNROLL, several, carry)
            return lax.fori_loop(count // UNROLL * UNROLL, count, step, carry)

        scores, prob_grad = products(last)
        key_at = lax.broadcasted_iota(jnp.int32, (KEYS, GROUP_ROWS), 0)
        row_at = lax.broadcasted_iota(jnp.int32, (KEYS, GROUP_ROWS), 1) & (ROWS - 1)
        scores = jnp.where(key_at <= row_at + (block - last * SPAN) * ROWS, scores, -1e30)
        base = highest(scores)
        total0, dot0 = keep(last, jnp.exp2(scores * EXP2_SCALE - base), prob_grad, base)

        def quick(j, carry):
            peak8, total8, dot8 = carry
            scores, prob_grad = products(j)
            total, dot = keep(j, jnp.exp2(scores * EXP2_SCALE - base), prob_grad, base)
            return jnp.maximum(peak8, fold(scores, jnp.max)), total8 + total, dot8 + dot

        peak8, total8, dot8 = unrolled(last, quick, (jnp.full((8, GROUP_ROWS), -1e30, F32), total0, dot0))
        stat_s[0:1] = base
        stat_s[8:16] = total8
        stat_s[16:24] = dot8

        @pl.when(jnp.max(peak8 * EXP2_SCALE - base) > HEADROOM)
        def _():
            def careful(j, carry):
                top, total8, dot8 = carry
                scores, prob_grad = products(j)
                new_top = jnp.maximum(top, highest(scores))
                total, dot = keep(j, jnp.exp2(scores * EXP2_SCALE - new_top), prob_grad, new_top)
                factor = jnp.exp2(top - new_top)
                return new_top, total8 * factor + total, dot8 * factor + dot

            top, total8, dot8 = lax.fori_loop(0, last, careful, (base, total0, dot0))
            stat_s[0:1] = top
            stat_s[8:16] = total8
            stat_s[16:24] = dot8

        top = stat_s[0:1]
        inverse = 1.0 / jnp.sum(stat_s[8:16], axis=0, keepdims=True)
        delta = jnp.sum(stat_s[16:24], axis=0, keepdims=True) * inverse
        dq_s[...] = jnp.zeros_like(dq_s)

        def backward(j, carry):
            probs = w_s[j] * (jnp.exp2(m_s[j][0:1] - top) * inverse)
            score_grad = (probs * (g_s[j] - delta)).astype(BF16)
            dv_s[j] += lax.dot_general(probs.astype(BF16), do[...], NN, preferred_element_type=F32)
            dk_s[j] += lax.dot_general(score_grad, q[...], NN, preferred_element_type=F32)
            columns = kt_s[:, pl.ds(pl.multiple_of(j * KEYS, KEYS), KEYS)]
            dq_s[...] += lax.dot_general(columns, score_grad, NN, preferred_element_type=F32)
            return carry

        unrolled(last + 1, backward, 0)
        for h in range(GROUP_ROWS // ROWS):
            part = dq_s[:, h * ROWS : (h + 1) * ROWS]
            q_s[group, h * ROWS : (h + 1) * ROWS, :] = (part.T * SCALE).astype(BF16)
        return 0

    lax.fori_loop(0, 2, one_group, 0)
    for n in range(2):
        for layer in range(LAYERS):
            for g in range(GROUPS):
                lo = layer * WIDTH + g * HEAD_DIM
                grad_refs[n * LAYERS + layer][:, g * HEAD_DIM : (g + 1) * HEAD_DIM] = q_s[n, lo : lo + ROWS, :]
    for j in range(CHUNKS):
        blocks = slice(j * SPAN, (j + 1) * SPAN)
        key_grad = dk_s[j] if first else dk_s[j] * SCALE
        term_ref[blocks, 0] = key_grad.astype(BF16).reshape(SPAN, ROWS, HEAD_DIM)
        term_ref[blocks, 1] = dv_s[j].astype(BF16).reshape(SPAN, ROWS, HEAD_DIM)


def attention(blocks, units, kv, sums=None):
    first = sums is None
    vmem = pl.BlockSpec(memory_space=pltpu.VMEM)
    args = [*units, kv] + ([] if first else [sums])
    return pl.pallas_call(
        functools.partial(attention_kernel, first),
        out_shape=[jax.ShapeDtypeStruct((ROWS, WIDTH), BF16)] * 4
        + [jax.ShapeDtypeStruct((BLOCKS, 2, ROWS, HEAD_DIM), BF16)],
        in_specs=[pl.BlockSpec(memory_space=pltpu.SMEM)] + [vmem] * len(args),
        out_specs=[vmem] * 5,
        scratch_shapes=[
            pltpu.VMEM((2, GROUP_ROWS, HEAD_DIM), BF16),
            pltpu.VMEM((2, GROUP_ROWS, HEAD_DIM), BF16),
            pltpu.VMEM((HEAD_DIM, BLOCKS * ROWS), BF16),
            pltpu.VMEM((CHUNKS, KEYS, GROUP_ROWS), F32),
            pltpu.VMEM((CHUNKS, KEYS, GROUP_ROWS), F32),
            pltpu.VMEM((CHUNKS, 8, GROUP_ROWS), F32),
            pltpu.VMEM((CHUNKS, KEYS, HEAD_DIM), F32),
            pltpu.VMEM((CHUNKS, KEYS, HEAD_DIM), F32),
            pltpu.VMEM((HEAD_DIM, GROUP_ROWS), F32),
            pltpu.VMEM((24, GROUP_ROWS), F32),
        ],
        compiler_params=pltpu.CompilerParams(vmem_limit_bytes=60 * 1024 * 1024),
        cost_estimate=pl.CostEstimate(flops=12_000_000_000, bytes_accessed=8_000_000, transcendentals=4_500_000),
        name="attention_first" if first else "attention_second",
    )(blocks, *args)


def spread_kernel(scales_ref, codes_ref, out_ref):
    for which in range(2):
        for part in range(ROWS // QUANT_BLOCK):
            rows = slice(part * QUANT_BLOCK, (part + 1) * QUANT_BLOCK)
            for head in range(2):
                codes = codes_ref[which, rows, head * HEAD_DIM : (head + 1) * HEAD_DIM].astype(F32)
                values = (codes * scales_ref[which, part, head]).astype(BF16)
                for to in range(16):
                    out_ref[head * 16 + to, which, rows, :] = values


def spread_cache(kv_codes, kv_scales):
    return pl.pallas_call(
        spread_kernel,
        out_shape=jax.ShapeDtypeStruct((BLOCKS, 2, ROWS, HEAD_DIM), BF16),
        in_specs=[pl.BlockSpec(memory_space=pltpu.SMEM), pl.BlockSpec(memory_space=pltpu.VMEM)],
        out_specs=pl.BlockSpec(memory_space=pltpu.VMEM),
        name="spread_cache",
    )(kv_scales, kv_codes)


CORE, FLIP, NEAR = 1, 2, 4
ACROSS = NEAR | FLIP


def partners(k):
    return [
        (s * BLOCKS + b, (s ^ (k & CORE) ^ (2 if k & NEAR else 0)) * BLOCKS + (flip(b) if k & FLIP else b))
        for s in range(4)
        for b in range(BLOCKS)
    ]


def move(x, k):
    return lax.ppermute(x, AXES, partners(k))


def shards(queries, out_grad, kv_codes, kv_scales):
    section, blk = lax.axis_index("section"), lax.axis_index("blk")
    head = section * 2 + blk // 16

    def of(k):
        return head ^ (4 if k & NEAR else 0) ^ (2 if k & CORE else 0) ^ (1 if k & FLIP else 0)

    kv = lax.all_to_all(spread_cache(kv_codes, kv_scales), "blk", 0, 0, tiled=True)

    def pick(k):
        at = of(k) * WIDTH
        return jnp.stack(
            [lax.dynamic_slice_in_dim(queries[0], at, WIDTH, 1), lax.dynamic_slice_in_dim(out_grad[0], at, WIDTH, 1)]
        )

    blocks = jnp.stack([blk, flip(blk)]).astype(jnp.int32)
    across = move(pick(ACROSS), ACROSS)
    across_core = move(pick(ACROSS | CORE), ACROSS | CORE)
    own, own_core = pick(0), move(pick(CORE), CORE)
    swapped = move(jnp.stack([pick(NEAR | CORE), pick(FLIP | CORE)]), CORE)
    near, turned = jnp.stack([pick(NEAR), swapped[0]]), jnp.stack([pick(FLIP), swapped[1]])
    near, turned, kv, across, across_core = lax.optimization_barrier((near, turned, kv, across, across_core))
    near, turned = move(near, NEAR), move(turned, FLIP)

    *first, sums = attention(blocks, (own, own_core, across, across_core), kv)
    near, turned, first[0] = lax.optimization_barrier((near, turned, first[0]))
    *second, term = attention(blocks, (near, turned), kv, sums)
    received = lax.all_to_all(term, "blk", 0, 0, tiled=True)
    grads = {}
    for k, grad in zip((0, CORE, ACROSS, ACROSS | CORE, NEAR, NEAR | CORE, FLIP, FLIP | CORE), first + second):
        grads[k] = move(grad, k) if k else grad

    kv_grad = received.reshape(2, 16, 2, ROWS, HEAD_DIM).astype(F32).sum(1)
    kv_grad = kv_grad.transpose(1, 2, 0, 3).reshape(2, ROWS, 2 * HEAD_DIM)
    query_grad = jnp.zeros((ROWS, 8 * WIDTH), BF16)
    for k, part in grads.items():
        query_grad = lax.dynamic_update_slice_in_dim(query_grad, part, of(k) * WIDTH, 1)
    return query_grad[None], kv_grad


def solution(mesh):
    in_specs = (
        P("section", "blk", None),
        P("section", "blk", None),
        P(None, "blk", "section"),
        P(None, "blk", "section"),
    )
    out_specs = (P("section", "blk", None), P(None, "blk", "section"))
    return jax.shard_map(shards, mesh=mesh, in_specs=in_specs, out_specs=out_specs, check_vma=False)
```

```python
import functools
import math

import jax
import jax.numpy as jnp
from jax import lax
from jax.experimental import pallas as pl
from jax.experimental.pallas import tpu as pltpu
from jax.sharding import PartitionSpec as P

HEAD_DIM = 128
GROUPS = 4
QUANT_BLOCK = 32
ROWS = 128
BLOCKS = 32
WIDTH = GROUPS * HEAD_DIM
AXES = ("section", "blk")
SCALE = 1.0 / math.sqrt(HEAD_DIM)
EXP2_SCALE = SCALE * math.log2(math.e)
F32 = jnp.float32
BF16 = jnp.bfloat16
NT = (((1,), (1,)), ((), ()))
NN = (((1,), (0,)), ((), ()))

LAYERS = 2
KEYS = 256
UNROLL = 4
SPAN = KEYS // ROWS
GROUP_ROWS = LAYERS * WIDTH
CHUNKS = BLOCKS // SPAN
HEADROOM = 64.0


def flip(blk):
    return blk ^ 30


def attention_kernel(first, blocks_ref, *refs):
    if first:
        units, refs = refs[:4], refs[4:]
    else:
        units, refs = [ref.at[layer] for ref in refs[:2] for layer in range(LAYERS)], refs[2:]
    kv_ref, refs = refs[0], refs[1:]
    if not first:
        sums_ref, refs = refs[0], refs[1:]
    *grad_refs, term_ref = refs[:-10]
    q_s, do_s, kt_s, w_s, g_s, m_s, dk_s, dv_s, dq_s, stat_s = refs[-10:]
    for n in range(2):
        for layer in range(LAYERS):
            unit = units[n * LAYERS + layer]
            for g in range(GROUPS):
                lo = layer * WIDTH + g * HEAD_DIM
                columns = slice(g * HEAD_DIM, (g + 1) * HEAD_DIM)
                q_s[n, lo : lo + ROWS, :] = unit[0, :, columns]
                do_s[n, lo : lo + ROWS, :] = unit[1, :, columns]
    for j in range(BLOCKS):
        kt_s[:, j * ROWS : (j + 1) * ROWS] = kv_ref[j, 0].T
    if first:
        dk_s[...] = jnp.zeros_like(dk_s)
        dv_s[...] = jnp.zeros_like(dv_s)
    else:
        for j in range(CHUNKS):
            blocks = slice(j * SPAN, (j + 1) * SPAN)
            dk_s[j] = sums_ref[blocks, 0].reshape(KEYS, HEAD_DIM).astype(F32)
            dv_s[j] = sums_ref[blocks, 1].reshape(KEYS, HEAD_DIM).astype(F32)

    def one_group(group, _):
        block = blocks_ref[group]
        last = block // SPAN
        q, do = q_s.at[group], do_s.at[group]

        def keys(j, which):
            return kv_ref[pl.ds(j * SPAN, SPAN), which].reshape(KEYS, HEAD_DIM)

        def fold(x, op):
            return op(x.reshape(KEYS // 8, 8, GROUP_ROWS), axis=0)

        def products(j):
            scores = lax.dot_general(keys(j, 0), q[...], NT, preferred_element_type=F32)
            return scores, lax.dot_general(keys(j, 1), do[...], NT, preferred_element_type=F32)

        def keep(j, weights, prob_grad, top):
            w_s[j] = weights.astype(BF16)
            g_s[j] = prob_grad
            m_s[j] = jnp.broadcast_to(top, (8, GROUP_ROWS))
            return fold(weights, jnp.sum), fold(weights * prob_grad, jnp.sum)

        def highest(scores):
            return jnp.max(fold(scores, jnp.max), axis=0, keepdims=True) * EXP2_SCALE

        def unrolled(count, step, carry):
            def several(t, carry):
                for n in range(UNROLL):
                    carry = step(t * UNROLL + n, carry)
                return carry

            carry = lax.fori_loop(0, count // UNROLL, several, carry)
            return lax.fori_loop(count // UNROLL * UNROLL, count, step, carry)

        scores, prob_grad = products(last)
        key_at = lax.broadcasted_iota(jnp.int32, (KEYS, GROUP_ROWS), 0)
        row_at = lax.broadcasted_iota(jnp.int32, (KEYS, GROUP_ROWS), 1) & (ROWS - 1)
        scores = jnp.where(key_at <= row_at + (block - last * SPAN) * ROWS, scores, -1e30)
        base = highest(scores)
        total0, dot0 = keep(last, jnp.exp2(scores * EXP2_SCALE - base), prob_grad, base)

        def quick(j, carry):
            peak8, total8, dot8 = carry
            scores, prob_grad = products(j)
            total, dot = keep(j, jnp.exp2(scores * EXP2_SCALE - base), prob_grad, base)
            return jnp.maximum(peak8, fold(scores, jnp.max)), total8 + total, dot8 + dot

        peak8, total8, dot8 = unrolled(last, quick, (jnp.full((8, GROUP_ROWS), -1e30, F32), total0, dot0))
        stat_s[0:1] = base
        stat_s[8:16] = total8
        stat_s[16:24] = dot8

        @pl.when(jnp.max(peak8 * EXP2_SCALE - base) > HEADROOM)
        def _():
            def careful(j, carry):
                top, total8, dot8 = carry
                scores, prob_grad = products(j)
                new_top = jnp.maximum(top, highest(scores))
                total, dot = keep(j, jnp.exp2(scores * EXP2_SCALE - new_top), prob_grad, new_top)
                factor = jnp.exp2(top - new_top)
                return new_top, total8 * factor + total, dot8 * factor + dot

            top, total8, dot8 = lax.fori_loop(0, last, careful, (base, total0, dot0))
            stat_s[0:1] = top
            stat_s[8:16] = total8
            stat_s[16:24] = dot8

        top = stat_s[0:1]
        inverse = 1.0 / jnp.sum(stat_s[8:16], axis=0, keepdims=True)
        delta = jnp.sum(stat_s[16:24], axis=0, keepdims=True) * inverse
        dq_s[...] = jnp.zeros_like(dq_s)

        def backward(j, carry):
            probs = w_s[j].astype(F32) * (jnp.exp2(m_s[j][0:1] - top) * inverse)
            score_grad = (probs * (g_s[j] - delta)).astype(BF16)
            dv_s[j] += lax.dot_general(probs.astype(BF16), do[...], NN, preferred_element_type=F32)
            dk_s[j] += lax.dot_general(score_grad, q[...], NN, preferred_element_type=F32)
            columns = kt_s[:, pl.ds(pl.multiple_of(j * KEYS, KEYS), KEYS)]
            dq_s[...] += lax.dot_general(columns, score_grad, NN, preferred_element_type=F32)
            return carry

        unrolled(last + 1, backward, 0)
        for h in range(GROUP_ROWS // ROWS):
            part = dq_s[:, h * ROWS : (h + 1) * ROWS]
            q_s[group, h * ROWS : (h + 1) * ROWS, :] = (part.T * SCALE).astype(BF16)
        return 0

    lax.fori_loop(0, 2, one_group, 0)
    for n in range(2):
        for layer in range(LAYERS):
            grad_ref = grad_refs[2].at[layer] if first and n else grad_refs[n * LAYERS + layer]
            for g in range(GROUPS):
                lo = layer * WIDTH + g * HEAD_DIM
                grad_ref[:, g * HEAD_DIM : (g + 1) * HEAD_DIM] = q_s[n, lo : lo + ROWS, :]
    for j in range(CHUNKS):
        blocks = slice(j * SPAN, (j + 1) * SPAN)
        key_grad = dk_s[j] if first else dk_s[j] * SCALE
        term_ref[blocks, 0] = key_grad.astype(BF16).reshape(SPAN, ROWS, HEAD_DIM)
        term_ref[blocks, 1] = dv_s[j].astype(BF16).reshape(SPAN, ROWS, HEAD_DIM)


def attention(blocks, units, kv, sums=None):
    first = sums is None
    vmem = pl.BlockSpec(memory_space=pltpu.VMEM)
    args = [*units, kv] + ([] if first else [sums])
    grad = jax.ShapeDtypeStruct((ROWS, WIDTH), BF16)
    pair = jax.ShapeDtypeStruct((LAYERS, ROWS, WIDTH), BF16)
    outs = [grad, grad, pair] if first else [grad] * 4
    outs.append(jax.ShapeDtypeStruct((BLOCKS, 2, ROWS, HEAD_DIM), BF16))
    return pl.pallas_call(
        functools.partial(attention_kernel, first),
        out_shape=outs,
        in_specs=[pl.BlockSpec(memory_space=pltpu.SMEM)] + [vmem] * len(args),
        out_specs=[vmem] * len(outs),
        scratch_shapes=[
            pltpu.VMEM((2, GROUP_ROWS, HEAD_DIM), BF16),
            pltpu.VMEM((2, GROUP_ROWS, HEAD_DIM), BF16),
            pltpu.VMEM((HEAD_DIM, BLOCKS * ROWS), BF16),
            pltpu.VMEM((CHUNKS, KEYS, GROUP_ROWS), BF16),
            pltpu.VMEM((CHUNKS, KEYS, GROUP_ROWS), F32),
            pltpu.VMEM((CHUNKS, 8, GROUP_ROWS), F32),
            pltpu.VMEM((CHUNKS, KEYS, HEAD_DIM), F32),
            pltpu.VMEM((CHUNKS, KEYS, HEAD_DIM), F32),
            pltpu.VMEM((HEAD_DIM, GROUP_ROWS), F32),
            pltpu.VMEM((24, GROUP_ROWS), F32),
        ],
        compiler_params=pltpu.CompilerParams(vmem_limit_bytes=42 * 1024 * 1024),
        cost_estimate=pl.CostEstimate(flops=12_000_000_000, bytes_accessed=8_000_000, transcendentals=4_500_000),
        name="attention_first" if first else "attention_second",
    )(blocks, *args)


def spread_kernel(scales_ref, codes_ref, out_ref):
    for which in range(2):
        for part in range(ROWS // QUANT_BLOCK):
            rows = slice(part * QUANT_BLOCK, (part + 1) * QUANT_BLOCK)
            for head in range(2):
                codes = codes_ref[which, rows, head * HEAD_DIM : (head + 1) * HEAD_DIM].astype(F32)
                scale = scales_ref[which, head : head + 1, part : part + 1]
                values = (codes * jnp.broadcast_to(scale, codes.shape)).astype(BF16)
                for to in range(16):
                    out_ref[head * 16 + to, which, rows, :] = values


def spread_cache(kv_codes, kv_scales):
    return pl.pallas_call(
        spread_kernel,
        out_shape=jax.ShapeDtypeStruct((BLOCKS, 2, ROWS, HEAD_DIM), BF16),
        in_specs=[pl.BlockSpec(memory_space=pltpu.VMEM)] * 2,
        out_specs=pl.BlockSpec(memory_space=pltpu.VMEM),
        name="spread_cache",
    )(kv_scales.transpose(0, 2, 1), kv_codes)


CORE, FLIP, NEAR = 1, 2, 4
ACROSS = NEAR | FLIP


def partners(k):
    return [
        (s * BLOCKS + b, (s ^ (k & CORE) ^ (2 if k & NEAR else 0)) * BLOCKS + (flip(b) if k & FLIP else b))
        for s in range(4)
        for b in range(BLOCKS)
    ]


def move(x, k):
    return lax.ppermute(x, AXES, partners(k))


def shards(queries, out_grad, kv_codes, kv_scales):
    section, blk = lax.axis_index("section"), lax.axis_index("blk")
    head = section * 2 + blk // 16

    def of(k):
        return head ^ (4 if k & NEAR else 0) ^ (2 if k & CORE else 0) ^ (1 if k & FLIP else 0)

    kv = lax.all_to_all(spread_cache(kv_codes, kv_scales), "blk", 0, 0, tiled=True)

    def pick(k):
        at = of(k) * WIDTH
        return jnp.stack(
            [lax.dynamic_slice_in_dim(queries[0], at, WIDTH, 1), lax.dynamic_slice_in_dim(out_grad[0], at, WIDTH, 1)]
        )

    blocks = jnp.stack([blk, flip(blk)]).astype(jnp.int32)
    across = move(pick(ACROSS), ACROSS)
    across_core = move(pick(ACROSS | CORE), ACROSS | CORE)
    own, own_core = pick(0), move(pick(CORE), CORE)
    swapped = move(jnp.stack([pick(NEAR | CORE), pick(FLIP | CORE)]), CORE)
    near, turned = jnp.stack([pick(NEAR), swapped[0]]), jnp.stack([pick(FLIP), swapped[1]])
    near, turned, kv, across, across_core = lax.optimization_barrier((near, turned, kv, across, across_core))
    near, turned = move(near, NEAR), move(turned, FLIP)

    d_own, d_own_core, d_across, sums = attention(blocks, (own, own_core, across, across_core), kv)
    d_across = move(d_across, ACROSS)
    *second, term = attention(blocks, (near, turned), kv, sums)
    d_across, term = lax.optimization_barrier((d_across, term))
    received = lax.all_to_all(term, "blk", 0, 0, tiled=True)
    grads = {0: d_own, CORE: move(d_own_core, CORE), ACROSS: d_across[0], ACROSS | CORE: move(d_across[1], CORE)}
    for k, grad in zip((NEAR, NEAR | CORE, FLIP, FLIP | CORE), second):
        grads[k] = move(grad, k)
    grads = lax.optimization_barrier(grads)
    kv_grad = received.reshape(2, 16, 2, ROWS, HEAD_DIM).astype(F32).sum(1)
    kv_grad = kv_grad.transpose(1, 2, 0, 3).reshape(2, ROWS, 2 * HEAD_DIM)
    query_grad = jnp.zeros((ROWS, 8 * WIDTH), BF16)
    for k, part in grads.items():
        query_grad = lax.dynamic_update_slice_in_dim(query_grad, part, of(k) * WIDTH, 1)
    return query_grad[None], kv_grad


def solution(mesh):
    in_specs = (
        P("section", "blk", None),
        P("section", "blk", None),
        P(None, "blk", "section"),
        P(None, "blk", "section"),
    )
    out_specs = (P("section", "blk", None), P(None, "blk", "section"))
    return jax.shard_map(shards, mesh=mesh, in_specs=in_specs, out_specs=out_specs, check_vma=False)
```

```python
import functools
import math

import jax
import jax.numpy as jnp
from jax import lax
from jax.experimental import pallas as pl
from jax.experimental.pallas import tpu as pltpu
from jax.sharding import PartitionSpec as P

HEAD_DIM = 128
GROUPS = 4
QUANT_BLOCK = 32
ROWS = 128
BLOCKS = 32
WIDTH = GROUPS * HEAD_DIM
AXES = ("section", "blk")
SCALE = 1.0 / math.sqrt(HEAD_DIM)
EXP2_SCALE = SCALE * math.log2(math.e)
F32 = jnp.float32
BF16 = jnp.bfloat16
NT = (((1,), (1,)), ((), ()))
NN = (((1,), (0,)), ((), ()))

LAYERS = 2
KEYS = 256
UNROLL = (6, 3, 1)
SPAN = KEYS // ROWS
GROUP_ROWS = LAYERS * WIDTH
CHUNKS = BLOCKS // SPAN
HEADROOM = 64.0


def flip(blk):
    return blk ^ 30


def attention_kernel(first, blocks_ref, *refs):
    if first:
        units, refs = refs[:4], refs[4:]
    else:
        units, refs = [ref.at[layer] for ref in refs[:2] for layer in range(LAYERS)], refs[2:]
    kv_ref, refs = refs[0], refs[1:]
    if not first:
        sums_ref, refs = refs[0], refs[1:]
    *grad_refs, term_ref = refs[:-10]
    q_s, do_s, kt_s, w_s, g_s, m_s, dk_s, dv_s, dq_s, stat_s = refs[-10:]
    for n in range(2):
        for layer in range(LAYERS):
            unit = units[n * LAYERS + layer]
            for g in range(GROUPS):
                lo = layer * WIDTH + g * HEAD_DIM
                columns = slice(g * HEAD_DIM, (g + 1) * HEAD_DIM)
                q_s[n, lo : lo + ROWS, :] = unit[0, :, columns]
                do_s[n, lo : lo + ROWS, :] = unit[1, :, columns]
    for j in range(BLOCKS):
        kt_s[:, j * ROWS : (j + 1) * ROWS] = kv_ref[j, 0].T
    if first:
        dk_s[...] = jnp.zeros_like(dk_s)
        dv_s[...] = jnp.zeros_like(dv_s)
    else:
        for j in range(CHUNKS):
            blocks = slice(j * SPAN, (j + 1) * SPAN)
            dk_s[j] = sums_ref[blocks, 0].reshape(KEYS, HEAD_DIM).astype(F32)
            dv_s[j] = sums_ref[blocks, 1].reshape(KEYS, HEAD_DIM).astype(F32)

    def one_group(group, _):
        block = blocks_ref[group]
        last = block // SPAN
        q, do = q_s.at[group], do_s.at[group]

        def keys(j, which):
            return kv_ref[pl.ds(j * SPAN, SPAN), which].reshape(KEYS, HEAD_DIM)

        def fold(x, op):
            return op(x.reshape(KEYS // 8, 8, GROUP_ROWS), axis=0)

        def products(j):
            scores = lax.dot_general(keys(j, 0), q[...], NT, preferred_element_type=F32)
            return scores, lax.dot_general(keys(j, 1), do[...], NT, preferred_element_type=F32)

        def keep(j, weights, prob_grad, top):
            w_s[j] = weights.astype(BF16)
            g_s[j] = prob_grad
            m_s[j] = jnp.broadcast_to(top, (8, GROUP_ROWS))
            return fold(weights, jnp.sum), fold(weights * prob_grad, jnp.sum)

        def highest(scores):
            return jnp.max(fold(scores, jnp.max), axis=0, keepdims=True) * EXP2_SCALE

        def unrolled(count, step, carry):
            def several(size, start, t, carry):
                for n in range(size):
                    carry = step(start + t * size + n, carry)
                return carry

            start = 0
            for size in UNROLL:
                times = (count - start) // size
                carry = lax.fori_loop(0, times, functools.partial(several, size, start), carry)
                start = start + times * size
            return carry

        scores, prob_grad = products(last)
        key_at = lax.broadcasted_iota(jnp.int32, (KEYS, GROUP_ROWS), 0)
        row_at = lax.broadcasted_iota(jnp.int32, (KEYS, GROUP_ROWS), 1) & (ROWS - 1)
        scores = jnp.where(key_at <= row_at + (block - last * SPAN) * ROWS, scores, -1e30)
        base = highest(scores)
        total0, dot0 = keep(last, jnp.exp2(scores * EXP2_SCALE - base), prob_grad, base)

        def quick(j, carry):
            peak8, total8, dot8 = carry
            scores, prob_grad = products(j)
            total, dot = keep(j, jnp.exp2(scores * EXP2_SCALE - base), prob_grad, base)
            return jnp.maximum(peak8, fold(scores, jnp.max)), total8 + total, dot8 + dot

        peak8, total8, dot8 = unrolled(last, quick, (jnp.full((8, GROUP_ROWS), -1e30, F32), total0, dot0))
        stat_s[0:1] = base
        stat_s[8:16] = total8
        stat_s[16:24] = dot8

        @pl.when(jnp.max(peak8 * EXP2_SCALE - base) > HEADROOM)
        def _():
            def careful(j, carry):
                top, total8, dot8 = carry
                scores, prob_grad = products(j)
                new_top = jnp.maximum(top, highest(scores))
                total, dot = keep(j, jnp.exp2(scores * EXP2_SCALE - new_top), prob_grad, new_top)
                factor = jnp.exp2(top - new_top)
                return new_top, total8 * factor + total, dot8 * factor + dot

            top, total8, dot8 = lax.fori_loop(0, last, careful, (base, total0, dot0))
            stat_s[0:1] = top
            stat_s[8:16] = total8
            stat_s[16:24] = dot8

        top = stat_s[0:1]
        inverse = 1.0 / jnp.sum(stat_s[8:16], axis=0, keepdims=True)
        delta = jnp.sum(stat_s[16:24], axis=0, keepdims=True) * inverse
        dq_s[...] = jnp.zeros_like(dq_s)

        def backward(j, carry):
            probs = w_s[j].astype(F32) * (jnp.exp2(m_s[j][0:1] - top) * inverse)
            score_grad = (probs * (g_s[j] - delta)).astype(BF16)
            dv_s[j] += lax.dot_general(probs.astype(BF16), do[...], NN, preferred_element_type=F32)
            dk_s[j] += lax.dot_general(score_grad, q[...], NN, preferred_element_type=F32)
            columns = kt_s[:, pl.ds(pl.multiple_of(j * KEYS, KEYS), KEYS)]
            dq_s[...] += lax.dot_general(columns, score_grad, NN, preferred_element_type=F32)
            return carry

        unrolled(last + 1, backward, 0)
        for h in range(GROUP_ROWS // ROWS):
            part = dq_s[:, h * ROWS : (h + 1) * ROWS]
            q_s[group, h * ROWS : (h + 1) * ROWS, :] = (part.T * SCALE).astype(BF16)
        return 0

    lax.fori_loop(0, 2, one_group, 0)
    for n in range(2):
        for layer in range(LAYERS):
            grad_ref = grad_refs[2].at[layer] if first and n else grad_refs[n * LAYERS + layer]
            for g in range(GROUPS):
                lo = layer * WIDTH + g * HEAD_DIM
                grad_ref[:, g * HEAD_DIM : (g + 1) * HEAD_DIM] = q_s[n, lo : lo + ROWS, :]
    for j in range(CHUNKS):
        blocks = slice(j * SPAN, (j + 1) * SPAN)
        key_grad = dk_s[j] if first else dk_s[j] * SCALE
        term_ref[blocks, 0] = key_grad.astype(BF16).reshape(SPAN, ROWS, HEAD_DIM)
        term_ref[blocks, 1] = dv_s[j].astype(BF16).reshape(SPAN, ROWS, HEAD_DIM)


def attention(blocks, units, kv, sums=None):
    first = sums is None
    vmem = pl.BlockSpec(memory_space=pltpu.VMEM)
    args = [*units, kv] + ([] if first else [sums])
    grad = jax.ShapeDtypeStruct((ROWS, WIDTH), BF16)
    pair = jax.ShapeDtypeStruct((LAYERS, ROWS, WIDTH), BF16)
    outs = [grad, grad, pair] if first else [grad] * 4
    outs.append(jax.ShapeDtypeStruct((BLOCKS, 2, ROWS, HEAD_DIM), BF16))
    return pl.pallas_call(
        functools.partial(attention_kernel, first),
        out_shape=outs,
        in_specs=[pl.BlockSpec(memory_space=pltpu.SMEM)] + [vmem] * len(args),
        out_specs=[vmem] * len(outs),
        scratch_shapes=[
            pltpu.VMEM((2, GROUP_ROWS, HEAD_DIM), BF16),
            pltpu.VMEM((2, GROUP_ROWS, HEAD_DIM), BF16),
            pltpu.VMEM((HEAD_DIM, BLOCKS * ROWS), BF16),
            pltpu.VMEM((CHUNKS, KEYS, GROUP_ROWS), BF16),
            pltpu.VMEM((CHUNKS, KEYS, GROUP_ROWS), F32),
            pltpu.VMEM((CHUNKS, 8, GROUP_ROWS), F32),
            pltpu.VMEM((CHUNKS, KEYS, HEAD_DIM), F32),
            pltpu.VMEM((CHUNKS, KEYS, HEAD_DIM), F32),
            pltpu.VMEM((HEAD_DIM, GROUP_ROWS), F32),
            pltpu.VMEM((24, GROUP_ROWS), F32),
        ],
        compiler_params=pltpu.CompilerParams(vmem_limit_bytes=42 * 1024 * 1024),
        cost_estimate=pl.CostEstimate(flops=12_000_000_000, bytes_accessed=8_000_000, transcendentals=4_500_000),
        name="attention_first" if first else "attention_second",
    )(blocks, *args)


def spread_kernel(scales_ref, codes_ref, out_ref):
    for which in range(2):
        for part in range(ROWS // QUANT_BLOCK):
            rows = slice(part * QUANT_BLOCK, (part + 1) * QUANT_BLOCK)
            for head in range(2):
                codes = codes_ref[which, rows, head * HEAD_DIM : (head + 1) * HEAD_DIM].astype(F32)
                scale = scales_ref[which, head : head + 1, part : part + 1]
                values = (codes * jnp.broadcast_to(scale, codes.shape)).astype(BF16)
                for to in range(16):
                    out_ref[head * 16 + to, which, rows, :] = values


def spread_cache(kv_codes, kv_scales):
    return pl.pallas_call(
        spread_kernel,
        out_shape=jax.ShapeDtypeStruct((BLOCKS, 2, ROWS, HEAD_DIM), BF16),
        in_specs=[pl.BlockSpec(memory_space=pltpu.VMEM)] * 2,
        out_specs=pl.BlockSpec(memory_space=pltpu.VMEM),
        name="spread_cache",
    )(kv_scales.transpose(0, 2, 1), kv_codes)


CORE, FLIP, NEAR = 1, 2, 4
ACROSS = NEAR | FLIP


def partners(k):
    return [
        (s * BLOCKS + b, (s ^ (k & CORE) ^ (2 if k & NEAR else 0)) * BLOCKS + (flip(b) if k & FLIP else b))
        for s in range(4)
        for b in range(BLOCKS)
    ]


def move(x, k):
    return lax.ppermute(x, AXES, partners(k))


def shards(queries, out_grad, kv_codes, kv_scales):
    section, blk = lax.axis_index("section"), lax.axis_index("blk")
    head = section * 2 + blk // 16

    def of(k):
        return head ^ (4 if k & NEAR else 0) ^ (2 if k & CORE else 0) ^ (1 if k & FLIP else 0)

    kv = lax.all_to_all(spread_cache(kv_codes, kv_scales), "blk", 0, 0, tiled=True)

    def pick(k):
        at = of(k) * WIDTH
        return jnp.stack(
            [lax.dynamic_slice_in_dim(queries[0], at, WIDTH, 1), lax.dynamic_slice_in_dim(out_grad[0], at, WIDTH, 1)]
        )

    blocks = jnp.stack([blk, flip(blk)]).astype(jnp.int32)
    across = move(pick(ACROSS), ACROSS)
    across_core = move(pick(ACROSS | CORE), ACROSS | CORE)
    own, own_core = pick(0), move(pick(CORE), CORE)
    swapped = move(jnp.stack([pick(NEAR | CORE), pick(FLIP | CORE)]), CORE)
    near, turned = jnp.stack([pick(NEAR), swapped[0]]), jnp.stack([pick(FLIP), swapped[1]])
    near, turned, kv, across, across_core = lax.optimization_barrier((near, turned, kv, across, across_core))
    near, turned = move(near, NEAR), move(turned, FLIP)

    d_own, d_own_core, d_across, sums = attention(blocks, (own, own_core, across, across_core), kv)
    d_across = move(d_across, ACROSS)
    *second, term = attention(blocks, (near, turned), kv, sums)
    d_across, term = lax.optimization_barrier((d_across, term))
    received = lax.all_to_all(term, "blk", 0, 0, tiled=True)
    grads = {0: d_own, CORE: move(d_own_core, CORE), ACROSS: d_across[0], ACROSS | CORE: move(d_across[1], CORE)}
    for k, grad in zip((NEAR, NEAR | CORE, FLIP, FLIP | CORE), second):
        grads[k] = move(grad, k)
    grads = lax.optimization_barrier(grads)
    kv_grad = received.reshape(2, 16, 2, ROWS, HEAD_DIM).astype(F32).sum(1)
    kv_grad = kv_grad.transpose(1, 2, 0, 3).reshape(2, ROWS, 2 * HEAD_DIM)
    query_grad = jnp.zeros((ROWS, 8 * WIDTH), BF16)
    for k, part in grads.items():
        query_grad = lax.dynamic_update_slice_in_dim(query_grad, part, of(k) * WIDTH, 1)
    return query_grad[None], kv_grad


def solution(mesh):
    in_specs = (
        P("section", "blk", None),
        P("section", "blk", None),
        P(None, "blk", "section"),
        P(None, "blk", "section"),
    )
    out_specs = (P("section", "blk", None), P(None, "blk", "section"))
    return jax.shard_map(shards, mesh=mesh, in_specs=in_specs, out_specs=out_specs, check_vma=False)
```

```python
import functools
import math

import jax
import jax.numpy as jnp
from jax import lax
from jax.experimental import pallas as pl
from jax.experimental.pallas import tpu as pltpu
from jax.sharding import PartitionSpec as P

HEAD_DIM = 128
GROUPS = 4
QUANT_BLOCK = 32
ROWS = 128
BLOCKS = 32
WIDTH = GROUPS * HEAD_DIM
AXES = ("section", "blk")
SCALE = 1.0 / math.sqrt(HEAD_DIM)
EXP2_SCALE = SCALE * math.log2(math.e)
F32 = jnp.float32
BF16 = jnp.bfloat16
NT = (((1,), (1,)), ((), ()))
NN = (((1,), (0,)), ((), ()))

LAYERS = 2
KEYS = 256
UNROLL = (6, 3, 1)
SPAN = KEYS // ROWS
GROUP_ROWS = LAYERS * WIDTH
CHUNKS = BLOCKS // SPAN
HEADROOM = 64.0


def flip(blk):
    return blk ^ 30


def attention_kernel(first, blocks_ref, *refs):
    if first:
        units, refs = refs[:4], refs[4:]
    else:
        units, refs = [*refs[:2], refs[2].at[0], refs[2].at[1]], refs[3:]
    kv_ref, refs = refs[0], refs[1:]
    if not first:
        sums_ref, refs = refs[0], refs[1:]
    *grad_refs, term_ref = refs[:-10]
    q_s, do_s, kt_s, w_s, g_s, m_s, dk_s, dv_s, dq_s, stat_s = refs[-10:]
    for n in range(2):
        for layer in range(LAYERS):
            unit = units[n * LAYERS + layer]
            for g in range(GROUPS):
                lo = layer * WIDTH + g * HEAD_DIM
                columns = slice(g * HEAD_DIM, (g + 1) * HEAD_DIM)
                q_s[n, lo : lo + ROWS, :] = unit[0, :, columns]
                do_s[n, lo : lo + ROWS, :] = unit[1, :, columns]
    for j in range(BLOCKS):
        kt_s[:, j * ROWS : (j + 1) * ROWS] = kv_ref[j, 0].T
    if first:
        dk_s[...] = jnp.zeros_like(dk_s)
        dv_s[...] = jnp.zeros_like(dv_s)
    else:
        for j in range(CHUNKS):
            blocks = slice(j * SPAN, (j + 1) * SPAN)
            dk_s[j] = sums_ref[blocks, 0].reshape(KEYS, HEAD_DIM).astype(F32)
            dv_s[j] = sums_ref[blocks, 1].reshape(KEYS, HEAD_DIM).astype(F32)

    def one_group(group, _):
        block = blocks_ref[group]
        last = block // SPAN
        q, do = q_s.at[group], do_s.at[group]

        def keys(j, which):
            return kv_ref[pl.ds(j * SPAN, SPAN), which].reshape(KEYS, HEAD_DIM)

        def fold(x, op):
            return op(x.reshape(KEYS // 8, 8, GROUP_ROWS), axis=0)

        def products(j):
            scores = lax.dot_general(keys(j, 0), q[...], NT, preferred_element_type=F32)
            return scores, lax.dot_general(keys(j, 1), do[...], NT, preferred_element_type=F32)

        def keep(j, weights, prob_grad, top):
            w_s[j] = weights.astype(BF16)
            g_s[j] = prob_grad
            m_s[j] = jnp.broadcast_to(top, (8, GROUP_ROWS))
            return fold(weights, jnp.sum), fold(weights * prob_grad, jnp.sum)

        def highest(scores):
            return jnp.max(fold(scores, jnp.max), axis=0, keepdims=True) * EXP2_SCALE

        def unrolled(count, step, carry):
            def several(size, start, t, carry):
                for n in range(size):
                    carry = step(start + t * size + n, carry)
                return carry

            start = 0
            for size in UNROLL:
                times = (count - start) // size
                carry = lax.fori_loop(0, times, functools.partial(several, size, start), carry)
                start = start + times * size
            return carry

        scores, prob_grad = products(last)
        key_at = lax.broadcasted_iota(jnp.int32, (KEYS, GROUP_ROWS), 0)
        row_at = lax.broadcasted_iota(jnp.int32, (KEYS, GROUP_ROWS), 1) & (ROWS - 1)
        scores = jnp.where(key_at <= row_at + (block - last * SPAN) * ROWS, scores, -1e30)
        base = highest(scores)
        total0, dot0 = keep(last, jnp.exp2(scores * EXP2_SCALE - base), prob_grad, base)

        def quick(j, carry):
            peak8, total8, dot8 = carry
            scores, prob_grad = products(j)
            total, dot = keep(j, jnp.exp2(scores * EXP2_SCALE - base), prob_grad, base)
            return jnp.maximum(peak8, fold(scores, jnp.max)), total8 + total, dot8 + dot

        peak8, total8, dot8 = unrolled(last, quick, (jnp.full((8, GROUP_ROWS), -1e30, F32), total0, dot0))
        stat_s[0:1] = base
        stat_s[8:16] = total8
        stat_s[16:24] = dot8

        @pl.when(jnp.max(peak8 * EXP2_SCALE - base) > HEADROOM)
        def _():
            def careful(j, carry):
                top, total8, dot8 = carry
                scores, prob_grad = products(j)
                new_top = jnp.maximum(top, highest(scores))
                total, dot = keep(j, jnp.exp2(scores * EXP2_SCALE - new_top), prob_grad, new_top)
                factor = jnp.exp2(top - new_top)
                return new_top, total8 * factor + total, dot8 * factor + dot

            top, total8, dot8 = lax.fori_loop(0, last, careful, (base, total0, dot0))
            stat_s[0:1] = top
            stat_s[8:16] = total8
            stat_s[16:24] = dot8

        top = stat_s[0:1]
        inverse = 1.0 / jnp.sum(stat_s[8:16], axis=0, keepdims=True)
        delta = jnp.sum(stat_s[16:24], axis=0, keepdims=True) * inverse
        dq_s[...] = jnp.zeros_like(dq_s)

        def backward(j, carry):
            probs = w_s[j].astype(F32) * (jnp.exp2(m_s[j][0:1] - top) * inverse)
            score_grad = (probs * (g_s[j] - delta)).astype(BF16)
            dv_s[j] += lax.dot_general(probs.astype(BF16), do[...], NN, preferred_element_type=F32)
            dk_s[j] += lax.dot_general(score_grad, q[...], NN, preferred_element_type=F32)
            columns = kt_s[:, pl.ds(pl.multiple_of(j * KEYS, KEYS), KEYS)]
            dq_s[...] += lax.dot_general(columns, score_grad, NN, preferred_element_type=F32)
            return carry

        unrolled(last + 1, backward, 0)
        for h in range(GROUP_ROWS // ROWS):
            part = dq_s[:, h * ROWS : (h + 1) * ROWS]
            q_s[group, h * ROWS : (h + 1) * ROWS, :] = (part.T * SCALE).astype(BF16)
        return 0

    lax.fori_loop(0, 2, one_group, 0)
    for n in range(2):
        for layer in range(LAYERS):
            grad_ref = grad_refs[n].at[layer] if first else grad_refs[n * LAYERS + layer]
            for g in range(GROUPS):
                lo = layer * WIDTH + g * HEAD_DIM
                grad_ref[:, g * HEAD_DIM : (g + 1) * HEAD_DIM] = q_s[n, lo : lo + ROWS, :]
    for j in range(CHUNKS):
        blocks = slice(j * SPAN, (j + 1) * SPAN)
        key_grad = dk_s[j] if first else dk_s[j] * SCALE
        term_ref[blocks, 0] = key_grad.astype(BF16).reshape(SPAN, ROWS, HEAD_DIM)
        term_ref[blocks, 1] = dv_s[j].astype(BF16).reshape(SPAN, ROWS, HEAD_DIM)


def attention(blocks, units, kv, sums=None):
    first = sums is None
    vmem = pl.BlockSpec(memory_space=pltpu.VMEM)
    args = [*units, kv] + ([] if first else [sums])
    grad = jax.ShapeDtypeStruct((ROWS, WIDTH), BF16)
    pair = jax.ShapeDtypeStruct((LAYERS, ROWS, WIDTH), BF16)
    outs = [pair, pair] if first else [grad] * 4
    outs.append(jax.ShapeDtypeStruct((BLOCKS, 2, ROWS, HEAD_DIM), BF16))
    return pl.pallas_call(
        functools.partial(attention_kernel, first),
        out_shape=outs,
        in_specs=[pl.BlockSpec(memory_space=pltpu.SMEM)] + [vmem] * len(args),
        out_specs=[vmem] * len(outs),
        scratch_shapes=[
            pltpu.VMEM((2, GROUP_ROWS, HEAD_DIM), BF16),
            pltpu.VMEM((2, GROUP_ROWS, HEAD_DIM), BF16),
            pltpu.VMEM((HEAD_DIM, BLOCKS * ROWS), BF16),
            pltpu.VMEM((CHUNKS, KEYS, GROUP_ROWS), BF16),
            pltpu.VMEM((CHUNKS, KEYS, GROUP_ROWS), F32),
            pltpu.VMEM((CHUNKS, 8, GROUP_ROWS), F32),
            pltpu.VMEM((CHUNKS, KEYS, HEAD_DIM), F32),
            pltpu.VMEM((CHUNKS, KEYS, HEAD_DIM), F32),
            pltpu.VMEM((HEAD_DIM, GROUP_ROWS), F32),
            pltpu.VMEM((24, GROUP_ROWS), F32),
        ],
        compiler_params=pltpu.CompilerParams(vmem_limit_bytes=42 * 1024 * 1024),
        cost_estimate=pl.CostEstimate(flops=12_000_000_000, bytes_accessed=8_000_000, transcendentals=4_500_000),
        name="attention_first" if first else "attention_second",
    )(blocks, *args)


def spread_kernel(scales_ref, codes_ref, out_ref):
    for which in range(2):
        for part in range(ROWS // QUANT_BLOCK):
            rows = slice(part * QUANT_BLOCK, (part + 1) * QUANT_BLOCK)
            for head in range(2):
                codes = codes_ref[which, rows, head * HEAD_DIM : (head + 1) * HEAD_DIM].astype(F32)
                scale = scales_ref[which, head : head + 1, part : part + 1]
                values = (codes * jnp.broadcast_to(scale, codes.shape)).astype(BF16)
                for to in range(16):
                    out_ref[head * 16 + to, which, rows, :] = values


def spread_cache(kv_codes, kv_scales):
    return pl.pallas_call(
        spread_kernel,
        out_shape=jax.ShapeDtypeStruct((BLOCKS, 2, ROWS, HEAD_DIM), BF16),
        in_specs=[pl.BlockSpec(memory_space=pltpu.VMEM)] * 2,
        out_specs=pl.BlockSpec(memory_space=pltpu.VMEM),
        name="spread_cache",
    )(kv_scales.transpose(0, 2, 1), kv_codes)


CORE, FLIP, NEAR = 1, 2, 4
ACROSS = NEAR | FLIP


def partners(k):
    return [
        (s * BLOCKS + b, (s ^ (k & CORE) ^ (2 if k & NEAR else 0)) * BLOCKS + (flip(b) if k & FLIP else b))
        for s in range(4)
        for b in range(BLOCKS)
    ]


def move(x, k):
    return lax.ppermute(x, AXES, partners(k))


def shards(queries, out_grad, kv_codes, kv_scales):
    section, blk = lax.axis_index("section"), lax.axis_index("blk")
    head = section * 2 + blk // 16

    def of(k):
        return head ^ (4 if k & NEAR else 0) ^ (2 if k & CORE else 0) ^ (1 if k & FLIP else 0)

    kv = lax.all_to_all(spread_cache(kv_codes, kv_scales), "blk", 0, 0, tiled=True)

    def pick(k):
        at = of(k) * WIDTH
        return jnp.stack(
            [lax.dynamic_slice_in_dim(queries[0], at, WIDTH, 1), lax.dynamic_slice_in_dim(out_grad[0], at, WIDTH, 1)]
        )

    blocks = jnp.stack([blk, flip(blk)]).astype(jnp.int32)
    near, near_core, turned, turned_core = [move(pick(k), k) for k in (NEAR, NEAR | CORE, FLIP, FLIP | CORE)]
    own, own_core = pick(0), move(pick(CORE), CORE)
    across = jnp.stack([pick(ACROSS), move(pick(ACROSS | CORE), CORE)])
    across, kv, near, near_core, turned, turned_core = lax.optimization_barrier(
        (across, kv, near, near_core, turned, turned_core)
    )
    across = move(across, ACROSS)

    d_near, d_turned, sums = attention(blocks, (near, near_core, turned, turned_core), kv)
    d_near, d_turned = move(d_near, NEAR), move(d_turned, FLIP)
    *second, term = attention(blocks, (own, own_core, across), kv, sums)
    d_near, d_turned, term = lax.optimization_barrier((d_near, d_turned, term))
    received = lax.all_to_all(term, "blk", 0, 0, tiled=True)
    grads = {NEAR: d_near[0], NEAR | CORE: move(d_near[1], CORE), FLIP: d_turned[0], FLIP | CORE: move(d_turned[1], CORE)}
    for k, grad in zip((0, CORE, ACROSS, ACROSS | CORE), second):
        grads[k] = move(grad, k) if k else grad
    grads = lax.optimization_barrier(grads)
    kv_grad = received.reshape(2, 16, 2, ROWS, HEAD_DIM).astype(F32).sum(1)
    kv_grad = kv_grad.transpose(1, 2, 0, 3).reshape(2, ROWS, 2 * HEAD_DIM)
    query_grad = jnp.zeros((ROWS, 8 * WIDTH), BF16)
    for k, part in grads.items():
        query_grad = lax.dynamic_update_slice_in_dim(query_grad, part, of(k) * WIDTH, 1)
    return query_grad[None], kv_grad


def solution(mesh):
    in_specs = (
        P("section", "blk", None),
        P("section", "blk", None),
        P(None, "blk", "section"),
        P(None, "blk", "section"),
    )
    out_specs = (P("section", "blk", None), P(None, "blk", "section"))
    return jax.shard_map(shards, mesh=mesh, in_specs=in_specs, out_specs=out_specs, check_vma=False)
```

```python
import functools
import math

import jax
import jax.numpy as jnp
from jax import lax
from jax.experimental import pallas as pl
from jax.experimental.pallas import tpu as pltpu
from jax.sharding import PartitionSpec as P

HEAD_DIM = 128
GROUPS = 4
QUANT_BLOCK = 32
ROWS = 128
BLOCKS = 32
WIDTH = GROUPS * HEAD_DIM
AXES = ("section", "blk")
SCALE = 1.0 / math.sqrt(HEAD_DIM)
EXP2_SCALE = SCALE * math.log2(math.e)
F32 = jnp.float32
BF16 = jnp.bfloat16
NT = (((1,), (1,)), ((), ()))
NN = (((1,), (0,)), ((), ()))

LAYERS = 2
KEYS = 256
UNROLL = (6, 3, 2, 1)
SPAN = KEYS // ROWS
GROUP_ROWS = LAYERS * WIDTH
CHUNKS = BLOCKS // SPAN
HEADROOM = 64.0


def flip(blk):
    return blk ^ 30


def attention_kernel(first, blocks_ref, *refs):
    if first:
        units, refs = refs[:4], refs[4:]
    else:
        units, refs = [*refs[:2], refs[2].at[0], refs[2].at[1]], refs[3:]
    kv_ref, refs = refs[0], refs[1:]
    if not first:
        sums_ref, refs = refs[0], refs[1:]
    *grad_refs, term_ref = refs[:-10]
    q_s, do_s, kt_s, w_s, g_s, m_s, dk_s, dv_s, dq_s, stat_s = refs[-10:]
    for n in range(2):
        for layer in range(LAYERS):
            unit = units[n * LAYERS + layer]
            for g in range(GROUPS):
                lo = layer * WIDTH + g * HEAD_DIM
                columns = slice(g * HEAD_DIM, (g + 1) * HEAD_DIM)
                q_s[n, lo : lo + ROWS, :] = unit[0, :, columns]
                do_s[n, lo : lo + ROWS, :] = unit[1, :, columns]
    for j in range(BLOCKS):
        kt_s[:, j * ROWS : (j + 1) * ROWS] = kv_ref[j, 0].T
    if first:
        dk_s[...] = jnp.zeros_like(dk_s)
        dv_s[...] = jnp.zeros_like(dv_s)
    else:
        for j in range(CHUNKS):
            blocks = slice(j * SPAN, (j + 1) * SPAN)
            dk_s[j] = sums_ref[blocks, 0].reshape(KEYS, HEAD_DIM).astype(F32)
            dv_s[j] = sums_ref[blocks, 1].reshape(KEYS, HEAD_DIM).astype(F32)

    def one_group(group, _):
        block = blocks_ref[group]
        last = block // SPAN
        q, do = q_s.at[group], do_s.at[group]

        def keys(j, which):
            return kv_ref[pl.ds(j * SPAN, SPAN), which].reshape(KEYS, HEAD_DIM)

        def fold(x, op):
            return op(x.reshape(KEYS // 8, 8, GROUP_ROWS), axis=0)

        def products(j):
            scores = lax.dot_general(keys(j, 0), q[...], NT, preferred_element_type=F32)
            return scores, lax.dot_general(keys(j, 1), do[...], NT, preferred_element_type=F32)

        def keep(j, weights, prob_grad, top):
            w_s[j] = weights.astype(BF16)
            g_s[j] = prob_grad
            m_s[j] = jnp.broadcast_to(top, (8, GROUP_ROWS))
            return fold(weights, jnp.sum), fold(weights * prob_grad, jnp.sum)

        def highest(scores):
            return jnp.max(fold(scores, jnp.max), axis=0, keepdims=True) * EXP2_SCALE

        def unrolled(count, step, carry):
            def several(size, start, t, carry):
                for n in range(size):
                    carry = step(start + t * size + n, carry)
                return carry

            start = 0
            for size in UNROLL:
                times = (count - start) // size
                carry = lax.fori_loop(0, times, functools.partial(several, size, start), carry)
                start = start + times * size
            return carry

        scores, prob_grad = products(last)
        key_at = lax.broadcasted_iota(jnp.int32, (KEYS, GROUP_ROWS), 0)
        row_at = lax.broadcasted_iota(jnp.int32, (KEYS, GROUP_ROWS), 1) & (ROWS - 1)
        scores = jnp.where(key_at <= row_at + (block - last * SPAN) * ROWS, scores, -1e30)
        base = highest(scores)
        total0, dot0 = keep(last, jnp.exp2(scores * EXP2_SCALE - base), prob_grad, base)

        def quick(j, carry):
            peak8, total8, dot8 = carry
            scores, prob_grad = products(j)
            total, dot = keep(j, jnp.exp2(scores * EXP2_SCALE - base), prob_grad, base)
            return jnp.maximum(peak8, fold(scores, jnp.max)), total8 + total, dot8 + dot

        peak8, total8, dot8 = unrolled(last, quick, (jnp.full((8, GROUP_ROWS), -1e30, F32), total0, dot0))
        stat_s[0:1] = base
        stat_s[8:16] = total8
        stat_s[16:24] = dot8

        @pl.when(jnp.max(peak8 * EXP2_SCALE - base) > HEADROOM)
        def _():
            def careful(j, carry):
                top, total8, dot8 = carry
                scores, prob_grad = products(j)
                new_top = jnp.maximum(top, highest(scores))
                total, dot = keep(j, jnp.exp2(scores * EXP2_SCALE - new_top), prob_grad, new_top)
                factor = jnp.exp2(top - new_top)
                return new_top, total8 * factor + total, dot8 * factor + dot

            top, total8, dot8 = lax.fori_loop(0, last, careful, (base, total0, dot0))
            stat_s[0:1] = top
            stat_s[8:16] = total8
            stat_s[16:24] = dot8

        top = stat_s[0:1]
        inverse = 1.0 / jnp.sum(stat_s[8:16], axis=0, keepdims=True)
        delta = jnp.sum(stat_s[16:24], axis=0, keepdims=True) * inverse
        dq_s[...] = jnp.zeros_like(dq_s)

        def backward(j, carry):
            probs = w_s[j].astype(F32) * (jnp.exp2(m_s[j][0:1] - top) * inverse)
            score_grad = (probs * (g_s[j] - delta)).astype(BF16)
            dv_s[j] += lax.dot_general(probs.astype(BF16), do[...], NN, preferred_element_type=F32)
            dk_s[j] += lax.dot_general(score_grad, q[...], NN, preferred_element_type=F32)
            columns = kt_s[:, pl.ds(pl.multiple_of(j * KEYS, KEYS), KEYS)]
            dq_s[...] += lax.dot_general(columns, score_grad, NN, preferred_element_type=F32)
            return carry

        unrolled(last + 1, backward, 0)
        for h in range(GROUP_ROWS // ROWS):
            part = dq_s[:, h * ROWS : (h + 1) * ROWS]
            q_s[group, h * ROWS : (h + 1) * ROWS, :] = (part.T * SCALE).astype(BF16)
        return 0

    lax.fori_loop(0, 2, one_group, 0)
    for n in range(2):
        for layer in range(LAYERS):
            grad_ref = grad_refs[n].at[layer] if first else grad_refs[n * LAYERS + layer]
            for g in range(GROUPS):
                lo = layer * WIDTH + g * HEAD_DIM
                grad_ref[:, g * HEAD_DIM : (g + 1) * HEAD_DIM] = q_s[n, lo : lo + ROWS, :]
    for j in range(CHUNKS):
        blocks = slice(j * SPAN, (j + 1) * SPAN)
        key_grad = dk_s[j] if first else dk_s[j] * SCALE
        term_ref[blocks, 0] = key_grad.astype(BF16).reshape(SPAN, ROWS, HEAD_DIM)
        term_ref[blocks, 1] = dv_s[j].astype(BF16).reshape(SPAN, ROWS, HEAD_DIM)


def attention(blocks, units, kv, sums=None):
    first = sums is None
    vmem = pl.BlockSpec(memory_space=pltpu.VMEM)
    args = [*units, kv] + ([] if first else [sums])
    grad = jax.ShapeDtypeStruct((ROWS, WIDTH), BF16)
    pair = jax.ShapeDtypeStruct((LAYERS, ROWS, WIDTH), BF16)
    outs = [pair, pair] if first else [grad] * 4
    outs.append(jax.ShapeDtypeStruct((BLOCKS, 2, ROWS, HEAD_DIM), BF16))
    return pl.pallas_call(
        functools.partial(attention_kernel, first),
        out_shape=outs,
        in_specs=[pl.BlockSpec(memory_space=pltpu.SMEM)] + [vmem] * len(args),
        out_specs=[vmem] * len(outs),
        scratch_shapes=[
            pltpu.VMEM((2, GROUP_ROWS, HEAD_DIM), BF16),
            pltpu.VMEM((2, GROUP_ROWS, HEAD_DIM), BF16),
            pltpu.VMEM((HEAD_DIM, BLOCKS * ROWS), BF16),
            pltpu.VMEM((CHUNKS, KEYS, GROUP_ROWS), BF16),
            pltpu.VMEM((CHUNKS, KEYS, GROUP_ROWS), F32),
            pltpu.VMEM((CHUNKS, 8, GROUP_ROWS), F32),
            pltpu.VMEM((CHUNKS, KEYS, HEAD_DIM), F32),
            pltpu.VMEM((CHUNKS, KEYS, HEAD_DIM), F32),
            pltpu.VMEM((HEAD_DIM, GROUP_ROWS), F32),
            pltpu.VMEM((24, GROUP_ROWS), F32),
        ],
        compiler_params=pltpu.CompilerParams(vmem_limit_bytes=46 * 1024 * 1024),
        cost_estimate=pl.CostEstimate(flops=12_000_000_000, bytes_accessed=8_000_000, transcendentals=4_500_000),
        name="attention_first" if first else "attention_second",
    )(blocks, *args)


def spread_kernel(scales_ref, codes_ref, out_ref):
    for which in range(2):
        for part in range(ROWS // QUANT_BLOCK):
            rows = slice(part * QUANT_BLOCK, (part + 1) * QUANT_BLOCK)
            for head in range(2):
                codes = codes_ref[which, rows, head * HEAD_DIM : (head + 1) * HEAD_DIM].astype(F32)
                scale = scales_ref[which, head : head + 1, part : part + 1]
                values = (codes * jnp.broadcast_to(scale, codes.shape)).astype(BF16)
                for to in range(16):
                    out_ref[head * 16 + to, which, rows, :] = values


def spread_cache(kv_codes, kv_scales):
    return pl.pallas_call(
        spread_kernel,
        out_shape=jax.ShapeDtypeStruct((BLOCKS, 2, ROWS, HEAD_DIM), BF16),
        in_specs=[pl.BlockSpec(memory_space=pltpu.VMEM)] * 2,
        out_specs=pl.BlockSpec(memory_space=pltpu.VMEM),
        name="spread_cache",
    )(kv_scales.transpose(0, 2, 1), kv_codes)


CORE, FLIP, NEAR = 1, 2, 4
ACROSS = NEAR | FLIP


def partners(k):
    return [
        (s * BLOCKS + b, (s ^ (k & CORE) ^ (2 if k & NEAR else 0)) * BLOCKS + (flip(b) if k & FLIP else b))
        for s in range(4)
        for b in range(BLOCKS)
    ]


def move(x, k):
    return lax.ppermute(x, AXES, partners(k))


def shards(queries, out_grad, kv_codes, kv_scales):
    section, blk = lax.axis_index("section"), lax.axis_index("blk")
    head = section * 2 + blk // 16

    def of(k):
        return head ^ (4 if k & NEAR else 0) ^ (2 if k & CORE else 0) ^ (1 if k & FLIP else 0)

    kv = lax.all_to_all(spread_cache(kv_codes, kv_scales), "blk", 0, 0, tiled=True)

    def pick(k):
        at = of(k) * WIDTH
        return jnp.stack(
            [lax.dynamic_slice_in_dim(queries[0], at, WIDTH, 1), lax.dynamic_slice_in_dim(out_grad[0], at, WIDTH, 1)]
        )

    blocks = jnp.stack([blk, flip(blk)]).astype(jnp.int32)
    near, near_core, turned, turned_core = [move(pick(k), k) for k in (NEAR, NEAR | CORE, FLIP, FLIP | CORE)]
    own, own_core = pick(0), move(pick(CORE), CORE)
    across = jnp.stack([pick(ACROSS), move(pick(ACROSS | CORE), CORE)])
    across, kv, near, near_core, turned, turned_core = lax.optimization_barrier(
        (across, kv, near, near_core, turned, turned_core)
    )
    across = move(across, ACROSS)

    d_near, d_turned, sums = attention(blocks, (near, near_core, turned, turned_core), kv)
    d_near, d_turned = move(d_near, NEAR), move(d_turned, FLIP)
    *second, term = attention(blocks, (own, own_core, across), kv, sums)
    d_near, d_turned, term = lax.optimization_barrier((d_near, d_turned, term))
    received = lax.all_to_all(term, "blk", 0, 0, tiled=True)
    grads = {NEAR: d_near[0], NEAR | CORE: move(d_near[1], CORE), FLIP: d_turned[0], FLIP | CORE: move(d_turned[1], CORE)}
    for k, grad in zip((0, CORE, ACROSS, ACROSS | CORE), second):
        grads[k] = move(grad, k) if k else grad
    grads = lax.optimization_barrier(grads)
    kv_grad = received.reshape(2, 16, 2, ROWS, HEAD_DIM).astype(F32).sum(1)
    kv_grad = kv_grad.transpose(1, 2, 0, 3).reshape(2, ROWS, 2 * HEAD_DIM)
    query_grad = jnp.zeros((ROWS, 8 * WIDTH), BF16)
    for k, part in grads.items():
        query_grad = lax.dynamic_update_slice_in_dim(query_grad, part, of(k) * WIDTH, 1)
    return query_grad[None], kv_grad


def solution(mesh):
    in_specs = (
        P("section", "blk", None),
        P("section", "blk", None),
        P(None, "blk", "section"),
        P(None, "blk", "section"),
    )
    out_specs = (P("section", "blk", None), P(None, "blk", "section"))
    return jax.shard_map(shards, mesh=mesh, in_specs=in_specs, out_specs=out_specs, check_vma=False)
```
